512 devices in a mesh: sample: 32 (over z_hi, y), space: 16 (over z_lo, x, core).
Axes of the slice: x: 4, y: 8, z: 8 (z_hi: 4, z_lo: 2; z = z_hi * 2 + z_lo), core: 2. Of those that a mesh axis runs over, the one named last changes fastest.
Arguments:
- feature_one: bfloat16 [32, 32, 64, 2048], P('sample', None, 'space'), may hold values from -6 to 6
- feature_two: bfloat16 [32, 64, 32, 512], P('sample', None, 'space'), may hold values from -6 to 6
- cotangent_three: bfloat16 [32, 128, 16, 128], P('sample', None, 'space'), may hold values from -6 to 6
- weight_two: bfloat16 [64, 864], replicated, may hold values from -0.625 to 0.625
- weight_three: bfloat16 [128, 1728], replicated, may hold values from -0.4375 to 0.4375
Outputs:
- cotangent_one: bfloat16 [32, 32, 64, 2048], P('sample', None, 'space')
- gradient_two: float32 [64, 864], P('space')
- gradient_three: float32 [128, 1728], P('space')
The draws below stay inside these ranges and needn't reach their ends.
All inputs are finite; a program needn't handle non-finite values.
Results may differ from the reference program's by a relative error of at most 0.008.
Values may be sent and summed in bfloat16 or wider, within the bound.
No kernel may reach another device: no remote copies, remote signals or barrier semaphores. Data moves between devices by JAX's collectives and lax.ppermute only.
A program may use at most 64 MiB of HBM per device.

```python
import jax
import jax.numpy as jnp
from jax import lax

C1 = 32
C2 = 64
C3 = 128
Y1 = 16
Z1 = 128
CUBES = 32
X1 = 64
X2 = 32
Y2 = 8
Z2 = 64
X3 = 16
Y3 = 4
Z3 = 32


def block_scale(own_key, shape, pieces, least, largest):
    factor_of, own = 1.0, jax.random.fold_in(own_key, 6)
    for dim, shards_of in pieces:
        steps = jnp.exp(jax.random.uniform(jax.random.fold_in(own, dim), (shards_of,), jnp.float32, least / len(pieces), largest / len(pieces)))
        factor_of = factor_of * jnp.repeat(steps, shape[dim] // shards_of).reshape([-1 if axis == dim else 1 for axis in range(len(shape))])
    return factor_of


def bell_draw(own_key, shape, width, most, cuts=(), dtype=jnp.bfloat16):
    drawn = width * jax.random.normal(own_key, shape, jnp.float32)
    if cuts:
        drawn = drawn * block_scale(own_key, shape, cuts, -0.22, 0.18)
    return jnp.clip(drawn, -most, most).astype(dtype)


def setup_inputs(seed: int = 0) -> dict:
    keys = jax.random.split(jax.random.key(seed), 6)
    return {
        "feature_one": bell_draw(keys[0], (CUBES, C1, X1, Y1 * Z1), 1.0, 6.0, ((0, 32), (2, 16))),
        "feature_two": bell_draw(keys[1], (CUBES, C2, X2, Y2 * Z2), 1.0, 6.0, ((0, 32), (2, 16))),
        "cotangent_three": bell_draw(keys[2], (CUBES, C3, X3, Y3 * Z3), 1.0, 6.0, ((0, 32), (2, 16))),
        "weight_two": bell_draw(keys[3], (C2, 27 * C1), (27 * C1 // 8) ** -0.5, 0.625),
        "weight_three": bell_draw(keys[4], (C3, 27 * C2), (27 * C2 // 8) ** -0.5, 0.4375),
    }


SLOPE = 0.3
PAIRS = ((slice(1, None), slice(1, None, 2)), (slice(0, -1), slice(0, None, 2)), (slice(0, -1), slice(1, None, 2)))
OPTIONS = (((1, 0),), ((2, 0), (0, 1)))


def leaky_slope(values):
    return jnp.where(values > 0, 1.0, SLOPE).astype(jnp.float32)


def weight_gradient(extended, acts):
    out_y, out_z = extended.shape[3], extended.shape[4]
    padded = jnp.pad(acts, ((0, 0), (0, 0), (0, 0), (1, 0), (1, 0)))
    blocks = []
    for a in range(3):
        grad_rows, act_rows = PAIRS[a]
        part = extended[:, :, grad_rows]
        flat_grad = part.reshape(part.shape[0], part.shape[1], -1)
        picked = padded[:, :, act_rows]
        for b in range(3):
            for c in range(3):
                window = picked[:, :, :, b:b + 2 * out_y:2, c:c + 2 * out_z:2]
                window = window.reshape(window.shape[0], window.shape[1], -1)
                blocks.append(jnp.einsum("bop,bcp->oc", flat_grad, window, preferred_element_type=jnp.float32))
    return jnp.concatenate(blocks, axis=1)


def data_gradient(extended, kernel, channels_in):
    taps = kernel.reshape(kernel.shape[0], 27, channels_in)
    batch, chans, ext_rows, out_y, out_z = extended.shape
    out_x = ext_rows - 1
    padded = jnp.pad(extended, ((0, 0), (0, 0), (0, 0), (0, 1), (0, 1)))
    planes = []
    for p in range(2):
        for q in range(2):
            for r in range(2):
                total = jnp.zeros((batch, channels_in, out_x * out_y * out_z), jnp.float32)
                for a, e in OPTIONS[p]:
                    for b, f in OPTIONS[q]:
                        for c, g in OPTIONS[r]:
                            window = padded[:, :, e:e + out_x, f:f + out_y, g:g + out_z].reshape(batch, chans, -1)
                            total = total + jnp.einsum("oc,bop->bcp", taps[:, a * 9 + b * 3 + c], window, preferred_element_type=jnp.float32)
                planes.append(total.reshape(batch, channels_in, out_x, out_y, out_z))
    stacked = jnp.stack(planes, axis=-1).reshape(batch, channels_in, out_x, out_y, out_z, 2, 2, 2)
    woven = stacked.transpose(0, 1, 2, 5, 3, 6, 4, 7)
    return woven.reshape(batch, channels_in, 2 * out_x, 2 * out_y, 2 * out_z)


def reference(feature_one, feature_two, cotangent_three, weight_two, weight_three):
    first = feature_one.reshape(CUBES, 1, C1, X1, Y1, Z1)
    second = feature_two.reshape(CUBES, 1, C2, X2, Y2, Z2)
    third = cotangent_three.reshape(CUBES, 1, C3, X3, Y3, Z3)

    def cube_step(carry, items):
        acts, middle, outer = items
        extended = jnp.concatenate([outer, jnp.zeros((1, C3, 1, Y3, Z3), jnp.bfloat16)], axis=2)
        grad_three = weight_gradient(extended, middle)
        back_two = (data_gradient(extended, weight_three, C2) * leaky_slope(middle)).astype(jnp.bfloat16)
        extended_two = jnp.concatenate([back_two, jnp.zeros((1, C2, 1, Y2, Z2), jnp.bfloat16)], axis=2)
        grad_two = weight_gradient(extended_two, acts)
        result = (data_gradient(extended_two, weight_two, C1) * leaky_slope(acts)).astype(jnp.bfloat16)
        return (carry[0] + grad_two, carry[1] + grad_three), result

    start = (jnp.zeros((C2, 27 * C1), jnp.float32), jnp.zeros((C3, 27 * C2), jnp.float32))
    sums, results = lax.scan(cube_step, start, (first, second, third))
    count = float(CUBES)
    return results.reshape(CUBES, C1, X1, Y1 * Z1), sums[0] / count, sums[1] / count
```

```python
import jax
import jax.numpy as jnp
import numpy as np
from jax import lax
from jax.experimental import pallas as pl
from jax.experimental.pallas import tpu as pltpu
from jax.sharding import Mesh
from jax.sharding import PartitionSpec as P

F32, BF16 = jnp.float32, jnp.bfloat16
SLOPE = 0.3
X1L, Y1, Z1 = 4, 16, 128
Y2, Z2 = 8, 64
Y3, Z3 = 4, 32
C1, C2, C3 = 32, 64, 128
L2, L3 = Y2 * Z2, Y3 * Z3
G2AT, SPLIT = 1792, 512
WIDTH = G2AT + SPLIT
CUBES = 32
TAP = {1: (0, 0), 2: (1, 0), 0: (1, 1)}


def class_matrix():
    m = np.zeros((L2, L2), np.float32)
    for y in range(Y2):
        for z in range(Z2):
            m[y * Z2 + z, ((y % 2) * 2 + z % 2) * L3 + (y // 2) * Z3 + z // 2] = 1
    return m


def shift_matrices():
    down = np.zeros((3, L3, L3), np.float32)
    for j in range(Y3):
        for k in range(Z3):
            for n, (dj, dk) in enumerate(((0, 1), (1, 0), (1, 1))):
                if j >= dj and k >= dk:
                    down[n, (j - dj) * Z3 + k - dk, j * Z3 + k] = 1
    up = down.transpose(0, 2, 1)
    return np.concatenate(list(down), 1), np.concatenate(list(up), 1)


def spread_matrix():
    m = np.zeros((2, Z2, 2, 3, Z1), np.float32)
    for h in range(2):
        for c in range(3):
            for k in range(Z2):
                z = 2 * k + c - 1
                if 0 <= z < Z1:
                    m[h, k, h, c, z] = 1
    return m.reshape(2 * Z2, 6 * Z1)


def pick_matrix():
    m = np.zeros((2, Z1, 3, 2, Z2), np.float32)
    for h in range(2):
        for c in range(3):
            for k in range(Z2):
                z = 2 * k + c - 1
                if 0 <= z < Z1:
                    m[h, z, c, h, k] = 1
    return m.reshape(2 * Z1, 6 * Z2)


def dot(a, b):
    return jnp.dot(a, b, preferred_element_type=F32)


def dot_nt(a, b):
    return lax.dot_general(a, b, (((1,), (1,)), ((), ())), preferred_element_type=F32)


def slope(v):
    return jnp.where(v.astype(F32) > 0, 1.0, SLOPE)


def kernel(cot, f2, f1, w3t, w2b, to_cls, to_nat, down, up, spread, pick,
           send, out, a3, cs, fw, we, wo, bu, bk4, g2s):
    cot_all = cot[...].reshape(2 * C3, L3)
    shifted = dot(cot_all, up[...]).astype(BF16)
    for row in range(2):
        lanes = pl.ds(row * L3, L3)
        cs[0:C3, lanes] = cot[row]
        for n in range(3):
            cs[(n + 1) * C3:(n + 2) * C3, lanes] = shifted[row * C3:(row + 1) * C3, n * L3:(n + 1) * L3]
    a3[...] = jnp.zeros_like(a3)
    for a in range(3):
        for b in range(3):
            for c in range(3):
                (q, f), (r, g) = TAP[b], TAP[c]
                rows, cols = (a * 4 + q * 2 + r) * C2, (f * 2 + g) * C3
                tap = (a * 9 + b * 3 + c) * C2
                a3[rows:rows + C2, cols:cols + C3] = w3t[tap:tap + C2, :]
    r3 = dot(a3[...], cs[...])
    n4 = 4 * C2
    totals = (r3[n4:2 * n4, :L3], r3[2 * n4:, :L3] + r3[:n4, L3:], r3[n4:2 * n4, L3:])
    f2c = dot(f2[...].reshape(3 * C2, L2), to_cls[...])
    back_cls = []
    for x in range(3):
        tiles = []
        for n in range(4):
            acts = f2c[x * C2:(x + 1) * C2, n * L3:(n + 1) * L3]
            tiles.append((totals[x][n * C2:(n + 1) * C2] * slope(acts)).astype(BF16))
        back_cls.append(jnp.concatenate(tiles, axis=1))
    back = dot(jnp.concatenate(back_cls, axis=0), to_nat[...]).astype(BF16)
    f2b = f2c[:2 * C2].astype(BF16)
    cls = [f2b[:, n * L3:(n + 1) * L3] for n in range(4)]
    moved = dot(cls[3], down[...]).astype(BF16)
    by_k, by_j, by_jk = moved[:, :L3], moved[:, L3:2 * L3], moved[:, 2 * L3:]
    row_k = dot(cls[1], down[:, :L3]).astype(BF16)
    col_j = dot(cls[2], down[:, L3:2 * L3]).astype(BF16)
    nine = (by_jk, col_j, by_j, row_k, cls[0], cls[1], by_k, cls[2], cls[3])
    win = [jnp.concatenate([w[x * C2:(x + 1) * C2] for w in nine], axis=0) for x in range(2)]
    send[:, :18 * C2] = dot_nt(cot[0], jnp.concatenate(win, axis=0)).astype(BF16)
    send[:, 18 * C2:27 * C2] = dot_nt(cot[1], win[1]).astype(BF16)
    for x in range(4):
        for b in range(3):
            for jp in range(4):
                rows = ((x * 3 + b) * 4 + jp) * C1
                y = 4 * jp + b - 1
                if y < 0:
                    fw[rows:rows + C1, :Z1] = jnp.zeros((C1, Z1), BF16)
                else:
                    fw[rows:rows + C1, :Z1] = f1[x, :, y * Z1:(y + 1) * Z1]
                fw[rows:rows + C1, Z1:] = f1[x, :, (y + 2) * Z1:(y + 3) * Z1]
    picked = dot(fw[...], pick[...]).astype(BF16)
    for x in range(4):
        dst = (we, wo)[x % 2]
        for b in range(3):
            for jp in range(4):
                rows = ((x * 3 + b) * 4 + jp) * C1
                lane = (x // 2) * L2 + jp * 2 * Z2
                for c in range(3):
                    at = (b * 3 + c) * C1
                    dst[at:at + C1, lane:lane + 2 * Z2] = picked[rows:rows + C1, c * 2 * Z2:(c + 1) * 2 * Z2]
    rows3 = [back[x * C2:(x + 1) * C2] for x in range(3)]
    pair = jnp.concatenate([jnp.concatenate([rows3[0], rows3[1]], 1), jnp.concatenate([rows3[1], rows3[2]], 1)], 0)
    even = dot_nt(pair[:C2], we[...])
    odd = dot_nt(pair, wo[...])
    grad = jnp.concatenate([odd[C2:], even, odd[:C2]], axis=1)
    g2s[...] = jnp.zeros_like(g2s)
    for s in range(C2 // 4):
        g2s[8 * s:8 * s + 4, :] = grad[4 * s:4 * s + 4, :SPLIT]
        g2s[8 * s + 4:8 * s + 8, :27 * C1 - SPLIT] = grad[4 * s:4 * s + 4, SPLIT:]
    send[:, 27 * C2:G2AT] = jnp.zeros((C3, G2AT - 27 * C2), BF16)
    send[:, G2AT:] = g2s[...].astype(BF16)
    for x in range(3):
        for jp in range(4):
            rows = (x * 4 + jp) * C2
            bk4[rows:rows + C2, :] = rows3[x][:, jp * 2 * Z2:(jp + 1) * 2 * Z2]
    wide = dot(bk4[...], spread[...]).astype(BF16)
    bu[:, Y2 * Z1:] = jnp.zeros((9 * C2, Z1), BF16)
    for x in range(3):
        for jp in range(4):
            for h in range(2):
                for c in range(3):
                    rows, at = (x * 4 + jp) * C2, (x * 3 + c) * C2
                    lane, col = (2 * jp + h) * Z1, (h * 3 + c) * Z1
                    bu[at:at + C2, lane:lane + Z1] = wide[rows:rows + C2, col:col + Z1]
    for i in range(2):
        ks = slice(i * 3 * C2, (i + 2) * 3 * C2)
        total = dot(w2b[0], bu[ks, :Y2 * Z1]) + dot(w2b[1], bu[ks, Z1:])
        for p in range(2):
            for q in range(2):
                for j in range(Y2):
                    lanes = pl.ds((2 * j + q) * Z1, Z1)
                    v = total[(p * 2 + q) * C1:(p * 2 + q + 1) * C1, j * Z1:(j + 1) * Z1]
                    out[2 * i + p, :, lanes] = (v * slope(f1[2 * i + p, :, lanes])).astype(BF16)


def main_call(cot, f2, f1, w3t, w2b):
    cls = class_matrix()
    down, up = shift_matrices()
    consts = [jnp.asarray(m, BF16) for m in (cls, cls.T, down, up, spread_matrix(), pick_matrix())]
    vm = pl.BlockSpec(memory_space=pltpu.VMEM)
    return pl.pallas_call(
        kernel,
        out_shape=(jax.ShapeDtypeStruct((C3, WIDTH), BF16), jax.ShapeDtypeStruct((X1L, C1, Y1 * Z1), BF16)),
        in_specs=[vm] * 11,
        out_specs=(vm, vm),
        scratch_shapes=[
            pltpu.VMEM((12 * C2, 4 * C3), BF16),
            pltpu.VMEM((4 * C3, 2 * L3), BF16),
            pltpu.VMEM((48 * C1, 2 * Z1), BF16),
            pltpu.VMEM((9 * C1, 2 * L2), BF16),
            pltpu.VMEM((9 * C1, 2 * L2), BF16),
            pltpu.VMEM((9 * C2, (Y2 + 1) * Z1), BF16),
            pltpu.VMEM((12 * C2, 2 * Z2), BF16),
            pltpu.VMEM((C3, SPLIT), F32),
        ],
        compiler_params=pltpu.CompilerParams(vmem_limit_bytes=48 * 1024 * 1024),
    )(cot, f2, f1, w3t, w2b, *consts)


def sum_kernel(got, sent):
    total = got[0].astype(F32)
    for n in range(1, got.shape[0]):
        total = total + got[n].astype(F32)
    total = total.astype(BF16)
    for n in range(sent.shape[0]):
        sent[n] = total


def summed_copies(got, copies):
    vm = pl.BlockSpec(memory_space=pltpu.VMEM)
    return pl.pallas_call(
        sum_kernel,
        out_shape=jax.ShapeDtypeStruct((copies,) + got.shape[1:], BF16),
        in_specs=[vm],
        out_specs=vm,
    )(got)


def last_kernel(got, two, three):
    total = got[0].astype(F32)
    for n in range(1, got.shape[0]):
        total = total + got[n].astype(F32)
    total = total * (1.0 / CUBES)
    three[:, 9 * C2:] = total[:, :18 * C2]
    three[:, :9 * C2] = total[:, 18 * C2:27 * C2]
    two[:, :SPLIT] = total[:4, G2AT:]
    two[:, SPLIT:] = total[4:, G2AT:G2AT + 27 * C1 - SPLIT]


def last_call(got):
    vm = pl.BlockSpec(memory_space=pltpu.VMEM)
    return pl.pallas_call(
        last_kernel,
        out_shape=(jax.ShapeDtypeStruct((4, 27 * C1), F32), jax.ShapeDtypeStruct((8, 27 * C2), F32)),
        in_specs=[vm],
        out_specs=(vm, vm),
    )(got)


def second_weights(weight):
    taps = weight.reshape(C2, 3, 3, 3, C1).transpose(1, 2, 4, 3, 0).reshape(3, 3, C1, 3 * C2)
    none = jnp.zeros((C1, 3 * C2), weight.dtype)
    tap_of = {v: k for k, v in TAP.items()}
    planes = []
    for f in range(2):
        rows = []
        for p in range(2):
            for q in range(2):
                cols = []
                for d in range(2):
                    a, b = tap_of.get((p, d)), tap_of.get((q, f))
                    cols.append(none if a is None or b is None else taps[a, b])
                rows.append(jnp.concatenate(cols, axis=1))
        planes.append(jnp.concatenate(rows, axis=0))
    return jnp.stack(planes)


def local(feature_one, feature_two, cotangent_three, weight_two, weight_three):
    cot = cotangent_three.reshape(C3, L3)
    f2 = feature_two.reshape(C2, 2, L2).transpose(1, 0, 2)
    count = lax.axis_size(SPACE)
    down = [(n, n - 1) for n in range(1, count)]
    above_cot = lax.ppermute(cot, SPACE, down)
    above_f2 = lax.ppermute(f2[0], SPACE, down)
    f1 = feature_one.reshape(C1, X1L, Y1 * Z1).transpose(1, 0, 2)
    cots = jnp.stack([cot, above_cot])
    f2s = jnp.concatenate([f2, above_f2[None]], axis=0)
    send, result = main_call(cots, f2s, f1, weight_three.T, second_weights(weight_two))
    got = lax.all_to_all(send.reshape(count, C3 // count, WIDTH), SPACE, 0, 0, tiled=True)
    got = lax.all_to_all(summed_copies(got, lax.axis_size("zh")), "zh", 0, 0, tiled=True)
    got = lax.all_to_all(summed_copies(got, lax.axis_size("y")), "y", 0, 0, tiled=True)
    two, three = last_call(got)
    return result.transpose(1, 0, 2).reshape(feature_one.shape), two, three


SPACE = ("zl", "x", "core")


def solution(mesh):
    samples = mesh.shape["sample"]
    inner = 8 if samples % 8 == 0 else 1
    fine = Mesh(mesh.devices.reshape(samples // inner, inner, 2, 4, 2), ("zh", "y") + SPACE)
    brick = P(("zh", "y"), None, SPACE, None)
    return jax.shard_map(
        local,
        mesh=fine,
        in_specs=(brick, brick, brick, P(), P()),
        out_specs=(brick, P(SPACE, None), P(SPACE, None)),
        check_vma=False,
    )
```

```python
import jax
import jax.numpy as jnp
import numpy as np
from jax import lax
from jax.experimental import pallas as pl
from jax.experimental.pallas import tpu as pltpu
from jax.sharding import Mesh
from jax.sharding import PartitionSpec as P

F32, BF16 = jnp.float32, jnp.bfloat16
SLOPE = 0.3
X1L, Y1, Z1 = 4, 16, 128
Y2, Z2 = 8, 64
Y3, Z3 = 4, 32
C1, C2, C3 = 32, 64, 128
L2, L3 = Y2 * Z2, Y3 * Z3
HALF = 27 * C1 // 2
WIDTH = 27 * C2 + HALF + 16
CUBES = 32
TAP = {1: (0, 0), 2: (1, 0), 0: (1, 1)}


def class_matrix():
    m = np.zeros((L2, L2), np.float32)
    for y in range(Y2):
        for z in range(Z2):
            m[y * Z2 + z, ((y % 2) * 2 + z % 2) * L3 + (y // 2) * Z3 + z // 2] = 1
    return m


def shift_matrices():
    down = np.zeros((3, L3, L3), np.float32)
    for j in range(Y3):
        for k in range(Z3):
            for n, (dj, dk) in enumerate(((0, 1), (1, 0), (1, 1))):
                if j >= dj and k >= dk:
                    down[n, (j - dj) * Z3 + k - dk, j * Z3 + k] = 1
    up = down.transpose(0, 2, 1)
    return np.concatenate(list(down), 1), np.concatenate(list(up), 1)


def spread_matrix():
    m = np.zeros((2, Z2, 2, 3, Z1), np.float32)
    for h in range(2):
        for c in range(3):
            for k in range(Z2):
                z = 2 * k + c - 1
                if 0 <= z < Z1:
                    m[h, k, h, c, z] = 1
    return m.reshape(2 * Z2, 6 * Z1)


def pick_matrix():
    m = np.zeros((2, Z1, 3, 2, Z2), np.float32)
    for h in range(2):
        for c in range(3):
            for k in range(Z2):
                z = 2 * k + c - 1
                if 0 <= z < Z1:
                    m[h, z, c, h, k] = 1
    return m.reshape(2 * Z1, 6 * Z2)


def dot(a, b):
    return jnp.dot(a, b, preferred_element_type=F32)


def dot_nt(a, b):
    return lax.dot_general(a, b, (((1,), (1,)), ((), ())), preferred_element_type=F32)


def slope(v):
    return jnp.where(v.astype(F32) > 0, 1.0, SLOPE)


def gradient_kernel(cot, f2, halo, f1, w3t, to_cls, to_nat, down, up, pick,
                    send, back_out, a3, cs, fw, we, wo, g2s):
    above = jnp.concatenate([halo[:, L2:L2 + L3], halo[:, L2 + L3:]], axis=0)
    cots = (cot[...], above)
    cot_all = jnp.concatenate(cots, axis=0)
    shifted = dot(cot_all, up[...]).astype(BF16)
    for row in range(2):
        lanes = pl.ds(row * L3, L3)
        cs[0:C3, lanes] = cots[row]
        for n in range(3):
            cs[(n + 1) * C3:(n + 2) * C3, lanes] = shifted[row * C3:(row + 1) * C3, n * L3:(n + 1) * L3]
    a3[...] = jnp.zeros_like(a3)
    for a in range(3):
        for b in range(3):
            for c in range(3):
                (q, f), (r, g) = TAP[b], TAP[c]
                rows, cols = (a * 4 + q * 2 + r) * C2, (f * 2 + g) * C3
                tap = (a * 9 + b * 3 + c) * C2
                a3[rows:rows + C2, cols:cols + C3] = w3t[tap:tap + C2, :]
    r3 = dot(a3[...], cs[...])
    n4 = 4 * C2
    totals = (r3[n4:2 * n4, :L3], r3[2 * n4:, :L3] + r3[:n4, L3:], r3[n4:2 * n4, L3:])
    f2c = dot(jnp.concatenate([f2[0], f2[1], halo[:, :L2]], axis=0), to_cls[...])
    back_cls = []
    for x in range(3):
        tiles = []
        for n in range(4):
            acts = f2c[x * C2:(x + 1) * C2, n * L3:(n + 1) * L3]
            tiles.append((totals[x][n * C2:(n + 1) * C2] * slope(acts)).astype(BF16))
        back_cls.append(jnp.concatenate(tiles, axis=1))
    back = dot(jnp.concatenate(back_cls, axis=0), to_nat[...]).astype(BF16)
    back_out[...] = back
    f2b = f2c[:2 * C2].astype(BF16)
    cls = [f2b[:, n * L3:(n + 1) * L3] for n in range(4)]
    moved = dot(cls[3], down[...]).astype(BF16)
    by_k, by_j, by_jk = moved[:, :L3], moved[:, L3:2 * L3], moved[:, 2 * L3:]
    row_k = dot(cls[1], down[:, :L3]).astype(BF16)
    col_j = dot(cls[2], down[:, L3:2 * L3]).astype(BF16)
    nine = (by_jk, col_j, by_j, row_k, cls[0], cls[1], by_k, cls[2], cls[3])
    win = [jnp.concatenate([w[x * C2:(x + 1) * C2] for w in nine], axis=0) for x in range(2)]
    by_tap = dot_nt(cots[0], jnp.concatenate(win, axis=0))
    by_tap_above = dot_nt(cots[1], win[1])
    for x in range(4):
        for b in range(3):
            for jp in range(4):
                rows = ((x * 3 + b) * 4 + jp) * C1
                y = 4 * jp + b - 1
                if y < 0:
                    fw[rows:rows + C1, :Z1] = jnp.zeros((C1, Z1), BF16)
                else:
                    fw[rows:rows + C1, :Z1] = f1[x, :, y * Z1:(y + 1) * Z1]
                fw[rows:rows + C1, Z1:] = f1[x, :, (y + 2) * Z1:(y + 3) * Z1]
    picked = dot(fw[...], pick[...]).astype(BF16)
    for x in range(4):
        dst = (we, wo)[x % 2]
        for b in range(3):
            for jp in range(4):
                rows = ((x * 3 + b) * 4 + jp) * C1
                lane = (x // 2) * L2 + jp * 2 * Z2
                for c in range(3):
                    at = (b * 3 + c) * C1
                    dst[at:at + C1, lane:lane + 2 * Z2] = picked[rows:rows + C1, c * 2 * Z2:(c + 1) * 2 * Z2]
    rows3 = [back[x * C2:(x + 1) * C2] for x in range(3)]
    pair = jnp.concatenate([jnp.concatenate([rows3[0], rows3[1]], 1), jnp.concatenate([rows3[1], rows3[2]], 1)], 0)
    even = dot_nt(pair[:C2], we[...])
    odd = dot_nt(pair, wo[...])
    grad = jnp.concatenate([odd[C2:], even, odd[:C2]], axis=1)
    first, second = grad[:, :HALF], grad[:, HALF:]
    for s in range(C2 // 4):
        g2s[8 * s:8 * s + 4, :] = first[4 * s:4 * s + 4]
        g2s[8 * s + 4:8 * s + 8, :] = second[4 * s:4 * s + 4]
    send[...] = jnp.concatenate(
        [by_tap_above, by_tap, g2s[...], jnp.zeros((C3, WIDTH - 27 * C2 - HALF), F32)], axis=1
    ).astype(BF16)


def activation_kernel(back, f1, w2b, spread, out, bu, bk4):
    rows3 = [back[x * C2:(x + 1) * C2, :] for x in range(3)]
    for x in range(3):
        for jp in range(4):
            rows = (x * 4 + jp) * C2
            bk4[rows:rows + C2, :] = rows3[x][:, jp * 2 * Z2:(jp + 1) * 2 * Z2]
    wide = dot(bk4[...], spread[...]).astype(BF16)
    bu[:, Y2 * Z1:] = jnp.zeros((9 * C2, Z1), BF16)
    for x in range(3):
        for jp in range(4):
            for h in range(2):
                for c in range(3):
                    rows, at = (x * 4 + jp) * C2, (x * 3 + c) * C2
                    lane, col = (2 * jp + h) * Z1, (h * 3 + c) * Z1
                    bu[at:at + C2, lane:lane + Z1] = wide[rows:rows + C2, col:col + Z1]
    for i in range(2):
        ks = slice(i * 3 * C2, (i + 2) * 3 * C2)
        total = dot(w2b[0], bu[ks, :Y2 * Z1]) + dot(w2b[1], bu[ks, Z1:])
        for p in range(2):
            for q in range(2):
                for j in range(Y2):
                    lanes = pl.ds((2 * j + q) * Z1, Z1)
                    v = total[(p * 2 + q) * C1:(p * 2 + q + 1) * C1, j * Z1:(j + 1) * Z1]
                    out[2 * i + p, :, lanes] = (v * slope(f1[2 * i + p, :, lanes])).astype(BF16)


VM = pl.BlockSpec(memory_space=pltpu.VMEM)
PARAMS = pltpu.CompilerParams(vmem_limit_bytes=32 * 1024 * 1024)


def gradients(cot, f2, halo, f1, w3t):
    cls = class_matrix()
    down, up = shift_matrices()
    consts = [jnp.asarray(m, BF16) for m in (cls, cls.T, down, up, pick_matrix())]
    return pl.pallas_call(
        gradient_kernel,
        out_shape=(jax.ShapeDtypeStruct((C3, WIDTH), BF16), jax.ShapeDtypeStruct((3 * C2, L2), BF16)),
        in_specs=[VM] * 10,
        out_specs=(VM, VM),
        scratch_shapes=[
            pltpu.VMEM((12 * C2, 4 * C3), BF16),
            pltpu.VMEM((4 * C3, 2 * L3), BF16),
            pltpu.VMEM((48 * C1, 2 * Z1), BF16),
            pltpu.VMEM((9 * C1, 2 * L2), BF16),
            pltpu.VMEM((9 * C1, 2 * L2), BF16),
            pltpu.VMEM((C3, HALF), F32),
        ],
        compiler_params=PARAMS,
        cost_estimate=pl.CostEstimate(flops=10**9, bytes_accessed=3 * 10**6, transcendentals=0),
    )(cot, f2, halo, f1, w3t, *consts)


def first_cotangent(back, f1, w2b):
    return pl.pallas_call(
        activation_kernel,
        out_shape=jax.ShapeDtypeStruct((X1L, C1, Y1 * Z1), BF16),
        in_specs=[VM] * 4,
        out_specs=VM,
        scratch_shapes=[
            pltpu.VMEM((9 * C2, (Y2 + 1) * Z1), BF16),
            pltpu.VMEM((12 * C2, 2 * Z2), BF16),
        ],
        compiler_params=PARAMS,
        cost_estimate=pl.CostEstimate(flops=2 * 10**9, bytes_accessed=6 * 10**6, transcendentals=0),
    )(back, f1, w2b, jnp.asarray(spread_matrix(), BF16))


def added(blocks):
    total = blocks[0].astype(F32)
    for n in range(1, blocks.shape[0]):
        total = total + blocks[n].astype(F32)
    return lax.optimization_barrier(total)


def summed_over(axis, part):
    count = lax.axis_size(axis)
    copies = jnp.broadcast_to(part.astype(BF16)[None], (count,) + part.shape)
    return added(lax.all_to_all(copies, axis, 0, 0, tiled=True))


def second_weights(weight):
    taps = weight.reshape(C2, 3, 3, 3, C1).transpose(1, 2, 4, 3, 0).reshape(3, 3, C1, 3 * C2)
    none = jnp.zeros((C1, 3 * C2), weight.dtype)
    tap_of = {v: k for k, v in TAP.items()}
    planes = []
    for f in range(2):
        rows = []
        for p in range(2):
            for q in range(2):
                cols = []
                for d in range(2):
                    a, b = tap_of.get((p, d)), tap_of.get((q, f))
                    cols.append(none if a is None or b is None else taps[a, b])
                rows.append(jnp.concatenate(cols, axis=1))
        planes.append(jnp.concatenate(rows, axis=0))
    return jnp.stack(planes)


def local(feature_one, feature_two, cotangent_three, weight_two, weight_three):
    cot = cotangent_three.reshape(C3, L3)
    f2 = feature_two.reshape(C2, 2, L2)
    count = lax.axis_size(SPACE)
    layer = jnp.concatenate([f2[:, 0], cot[:C2], cot[C2:]], axis=1)
    halo = lax.ppermute(layer, SPACE, [(n, n - 1) for n in range(1, count)])
    f1 = feature_one.reshape(C1, X1L, Y1 * Z1).transpose(1, 0, 2)
    send, back = gradients(cot, f2.transpose(1, 0, 2), halo, f1, weight_three.T)
    got = lax.all_to_all(send.reshape(count, C3 // count, WIDTH), SPACE, 0, 0, tiled=True)
    result = first_cotangent(back, f1, second_weights(weight_two))
    total = summed_over("y", summed_over("zh", added(got))) * (1.0 / CUBES)
    three = total[:, :27 * C2]
    two = jnp.concatenate([total[:4, 27 * C2:27 * C2 + HALF], total[4:, 27 * C2:27 * C2 + HALF]], axis=1)
    return result.transpose(1, 0, 2).reshape(feature_one.shape), two, three


SPACE = ("zl", "x", "core")


def solution(mesh):
    samples = mesh.shape["sample"]
    inner = 8 if samples % 8 == 0 else 1
    fine = Mesh(mesh.devices.reshape(samples // inner, inner, 2, 4, 2), ("zh", "y") + SPACE)
    brick = P(("zh", "y"), None, SPACE, None)
    return jax.shard_map(
        local,
        mesh=fine,
        in_specs=(brick, brick, brick, P(), P()),
        out_specs=(brick, P(SPACE, None), P(SPACE, None)),
        check_vma=False,
    )
```

```python
import jax
import jax.numpy as jnp
import numpy as np
from jax import lax
from jax.experimental import pallas as pl
from jax.experimental.pallas import tpu as pltpu
from jax.sharding import Mesh
from jax.sharding import PartitionSpec as P

F32, BF16 = jnp.float32, jnp.bfloat16
SLOPE = 0.3
X1L, Y1, Z1 = 4, 16, 128
Y2, Z2 = 8, 64
Y3, Z3 = 4, 32
C1, C2, C3 = 32, 64, 128
L2, L3 = Y2 * Z2, Y3 * Z3
HALF = 27 * C1 // 2
WIDTH = 27 * C2 + HALF + 16
CUBES = 32
TAP = {1: (0, 0), 2: (1, 0), 0: (1, 1)}


def class_matrix():
    m = np.zeros((L2, L2), np.float32)
    for y in range(Y2):
        for z in range(Z2):
            m[y * Z2 + z, ((y % 2) * 2 + z % 2) * L3 + (y // 2) * Z3 + z // 2] = 1
    return m


def shift_matrices():
    down = np.zeros((3, L3, L3), np.float32)
    for j in range(Y3):
        for k in range(Z3):
            for n, (dj, dk) in enumerate(((0, 1), (1, 0), (1, 1))):
                if j >= dj and k >= dk:
                    down[n, (j - dj) * Z3 + k - dk, j * Z3 + k] = 1
    up = down.transpose(0, 2, 1)
    return np.concatenate(list(down), 1), np.concatenate(list(up), 1)


def spread_matrix():
    m = np.zeros((2, Z2, 2, 3, Z1), np.float32)
    for h in range(2):
        for c in range(3):
            for k in range(Z2):
                z = 2 * k + c - 1
                if 0 <= z < Z1:
                    m[h, k, h, c, z] = 1
    return m.reshape(2 * Z2, 6 * Z1)


def pick_matrix():
    m = np.zeros((2, Z1, 3, 2, Z2), np.float32)
    for h in range(2):
        for c in range(3):
            for k in range(Z2):
                z = 2 * k + c - 1
                if 0 <= z < Z1:
                    m[h, z, c, h, k] = 1
    return m.reshape(2 * Z1, 6 * Z2)


def dot(a, b):
    return jnp.dot(a, b, preferred_element_type=F32)


def dot_nt(a, b):
    return lax.dot_general(a, b, (((1,), (1,)), ((), ())), preferred_element_type=F32)


def slope(v):
    return jnp.where(v.astype(F32) > 0, 1.0, SLOPE)


def prepare_kernel(cot, f2, layer, f2_rows, held, sems):
    copies = [
        pltpu.make_async_copy(f2, held, sems.at[0]),
        pltpu.make_async_copy(cot.at[:C2], layer.at[:, L2:L2 + L3], sems.at[1]),
        pltpu.make_async_copy(cot.at[C2:], layer.at[:, L2 + L3:], sems.at[2]),
    ]
    for copy in copies:
        copy.start()
    copies[0].wait()
    top = held[:, 0, :]
    layer[:, :L2] = top
    f2_rows[:C2, :] = top
    f2_rows[C2:, :] = held[:, 1, :]
    copies[1].wait()
    copies[2].wait()


def shifts(values, matrices, dst):
    moved = dot(values, matrices).astype(BF16)
    dst[0:C3, :] = values
    for n in range(3):
        dst[(n + 1) * C3:(n + 2) * C3, :] = moved[:, n * L3:(n + 1) * L3]


def own_kernel(cot, f2, f1, w3t, to_cls, small,
               by_tap, totals, act_cls, win_odd, we, wo, a3, cs, fw):
    down, up, pick = small[:L3, :], small[L3:2 * L3, :], small[2 * L3:, :]
    shifts(cot[...], up, cs)
    a3[...] = jnp.zeros_like(a3)
    for a in range(3):
        for b in range(3):
            for c in range(3):
                (q, f), (r, g) = TAP[b], TAP[c]
                rows, cols = (a * 4 + q * 2 + r) * C2, (f * 2 + g) * C3
                tap = (a * 9 + b * 3 + c) * C2
                a3[rows:rows + C2, cols:cols + C3] = w3t[tap:tap + C2, :]
    totals[...] = dot(a3[4 * C2:, :], cs[...])
    f2b = dot(f2[...], to_cls[...]).astype(BF16)
    act_cls[...] = f2b
    cls = [f2b[:, n * L3:(n + 1) * L3] for n in range(4)]
    moved = dot(cls[3], down).astype(BF16)
    by_k, by_j, by_jk = moved[:, :L3], moved[:, L3:2 * L3], moved[:, 2 * L3:]
    row_k = dot(cls[1], down[:, :L3]).astype(BF16)
    col_j = dot(cls[2], down[:, L3:2 * L3]).astype(BF16)
    nine = (by_jk, col_j, by_j, row_k, cls[0], cls[1], by_k, cls[2], cls[3])
    win = [jnp.concatenate([w[x * C2:(x + 1) * C2] for w in nine], axis=0) for x in range(2)]
    win_odd[...] = win[1]
    by_tap[...] = dot_nt(cot[...], jnp.concatenate(win, axis=0)).astype(BF16)
    for x in range(4):
        for b in range(3):
            for jp in range(4):
                rows = ((x * 3 + b) * 4 + jp) * C1
                y = 4 * jp + b - 1
                if y < 0:
                    fw[rows:rows + C1, :Z1] = jnp.zeros((C1, Z1), BF16)
                else:
                    fw[rows:rows + C1, :Z1] = f1[x, :, y * Z1:(y + 1) * Z1]
                fw[rows:rows + C1, Z1:] = f1[x, :, (y + 2) * Z1:(y + 3) * Z1]
    picked = dot(fw[...], pick).astype(BF16)
    for x in range(4):
        dst = (we, wo)[x % 2]
        for b in range(3):
            for jp in range(4):
                rows = ((x * 3 + b) * 4 + jp) * C1
                lane = (x // 2) * L2 + jp * 2 * Z2
                for c in range(3):
                    at = (b * 3 + c) * C1
                    dst[at:at + C1, lane:lane + 2 * Z2] = picked[rows:rows + C1, c * 2 * Z2:(c + 1) * 2 * Z2]


def joined_kernel(halo, by_tap, totals, act_cls, win_odd, we, wo, a3, to_cls, to_nat, small,
                  send, back_out, cs, g2s):
    up = small[L3:2 * L3, :]
    above = jnp.concatenate([halo[:, L2:L2 + L3], halo[:, L2 + L3:]], axis=0)
    shifts(above, up, cs)
    n4 = 4 * C2
    over = dot(a3[:2 * n4, :], cs[...])
    sums = (totals[:n4, :], totals[n4:, :] + over[:n4], over[n4:])
    above_cls = dot(halo[:, :L2], to_cls[...])
    acts = (act_cls[:C2, :], act_cls[C2:, :], above_cls)
    back_cls = []
    for x in range(3):
        tiles = []
        for n in range(4):
            gain = slope(acts[x][:, n * L3:(n + 1) * L3])
            tiles.append((sums[x][n * C2:(n + 1) * C2] * gain).astype(BF16))
        back_cls.append(jnp.concatenate(tiles, axis=1))
    back = dot(jnp.concatenate(back_cls, axis=0), to_nat[...]).astype(BF16)
    back_out[...] = back
    by_tap_above = dot_nt(above, win_odd[...])
    rows3 = [back[x * C2:(x + 1) * C2] for x in range(3)]
    pair = jnp.concatenate([jnp.concatenate([rows3[0], rows3[1]], 1), jnp.concatenate([rows3[1], rows3[2]], 1)], 0)
    even = dot_nt(pair[:C2], we[...])
    odd = dot_nt(pair, wo[...])
    grad = jnp.concatenate([odd[C2:], even, odd[:C2]], axis=1)
    first, second = grad[:, :HALF], grad[:, HALF:]
    for s in range(C2 // 4):
        g2s[8 * s:8 * s + 4, :] = first[4 * s:4 * s + 4]
        g2s[8 * s + 4:8 * s + 8, :] = second[4 * s:4 * s + 4]
    send[:, :18 * C2] = by_tap[...]
    send[:, 18 * C2:] = jnp.concatenate(
        [by_tap_above, g2s[...], jnp.zeros((C3, WIDTH - 27 * C2 - HALF), F32)], axis=1
    ).astype(BF16)


def activation_kernel(back, f1, w2, spread, out, bu, bk4, w2x):
    rows3 = [back[x * C2:(x + 1) * C2, :] for x in range(3)]
    w2x[...] = jnp.zeros_like(w2x)
    for a in range(3):
        for b in range(3):
            for c in range(3):
                (p, d), (q, f) = TAP[a], TAP[b]
                rows, cols = (d * 3 + c) * C2, (p * 2 + q) * C1
                tap = (a * 9 + b * 3 + c) * C1
                w2x[f, rows:rows + C2, cols:cols + C1] = w2[:, tap:tap + C1].astype(F32)
    w2b = [w2x[f].T.astype(BF16) for f in range(2)]
    for x in range(3):
        for jp in range(4):
            rows = (x * 4 + jp) * C2
            bk4[rows:rows + C2, :] = rows3[x][:, jp * 2 * Z2:(jp + 1) * 2 * Z2]
    wide = dot(bk4[...], spread[...]).astype(BF16)
    bu[:, Y2 * Z1:] = jnp.zeros((9 * C2, Z1), BF16)
    for x in range(3):
        for jp in range(4):
            for h in range(2):
                for c in range(3):
                    rows, at = (x * 4 + jp) * C2, (x * 3 + c) * C2
                    lane, col = (2 * jp + h) * Z1, (h * 3 + c) * Z1
                    bu[at:at + C2, lane:lane + Z1] = wide[rows:rows + C2, col:col + Z1]
    for i in range(2):
        ks = slice(i * 3 * C2, (i + 2) * 3 * C2)
        total = dot(w2b[0], bu[ks, :Y2 * Z1]) + dot(w2b[1], bu[ks, Z1:])
        for p in range(2):
            for q in range(2):
                for j in range(Y2):
                    lanes = pl.ds((2 * j + q) * Z1, Z1)
                    v = total[(p * 2 + q) * C1:(p * 2 + q + 1) * C1, j * Z1:(j + 1) * Z1]
                    out[2 * i + p, :, lanes] = (v * slope(f1[2 * i + p, :, lanes])).astype(BF16)


VM = pl.BlockSpec(memory_space=pltpu.VMEM)


def call(body, args, outs, scratch=(), flops=10**8, moved=10**6, limit=24, source=VM):
    return pl.pallas_call(
        body,
        out_shape=tuple(jax.ShapeDtypeStruct(shape, dtype) for shape, dtype in outs),
        in_specs=[source] * len(args),
        out_specs=(VM,) * len(outs),
        scratch_shapes=list(scratch),
        compiler_params=pltpu.CompilerParams(vmem_limit_bytes=limit * 1024 * 1024),
        cost_estimate=pl.CostEstimate(flops=flops, bytes_accessed=moved, transcendentals=0),
    )(*args)


def last_kernel(got, two, three):
    total = got[0].astype(F32)
    for n in range(1, got.shape[0]):
        total = total + got[n].astype(F32)
    total = total * (1.0 / CUBES)
    three[:, 9 * C2:] = total[:, :18 * C2]
    three[:, :9 * C2] = total[:, 18 * C2:27 * C2]
    two[...] = jnp.concatenate([total[:4, 27 * C2:27 * C2 + HALF], total[4:, 27 * C2:27 * C2 + HALF]], axis=1)


def added(blocks):
    total = blocks[0].astype(F32)
    for n in range(1, blocks.shape[0]):
        total = total + blocks[n].astype(F32)
    return lax.optimization_barrier(total)


def from_all(axis, part):
    count = lax.axis_size(axis)
    copies = jnp.broadcast_to(part.astype(BF16)[None], (count,) + part.shape)
    return lax.all_to_all(copies, axis, 0, 0, tiled=True)


def local(feature_one, feature_two, cotangent_three, weight_two, weight_three):
    count = lax.axis_size(SPACE)
    cls = class_matrix()
    to_cls, to_nat = jnp.asarray(cls, BF16), jnp.asarray(cls.T, BF16)
    small = jnp.asarray(np.concatenate(shift_matrices() + (pick_matrix(),), 0), BF16)
    cot = cotangent_three.reshape(C3, L3)
    layer, f2 = call(
        prepare_kernel, (cot, feature_two.reshape(C2, 2, L2)),
        (((C2, L2 + 2 * L3), BF16), ((2 * C2, L2), BF16)), (pltpu.VMEM((C2, 2, L2), BF16), pltpu.SemaphoreType.DMA((3,))),
        limit=4, source=pl.BlockSpec(memory_space=pltpu.HBM),
    )
    halo = lax.ppermute(layer, SPACE, [(n, n - 1) for n in range(1, count)])
    f1 = feature_one.reshape(C1, X1L, Y1 * Z1).transpose(1, 0, 2)
    own = call(
        own_kernel, (cot, f2, f1, weight_three.T, to_cls, small),
        (((C3, 18 * C2), BF16), ((8 * C2, L3), F32), ((2 * C2, L2), BF16), ((9 * C2, L3), BF16),
         ((9 * C1, 2 * L2), BF16), ((9 * C1, 2 * L2), BF16), ((12 * C2, 4 * C3), BF16)),
        (pltpu.VMEM((4 * C3, L3), BF16), pltpu.VMEM((48 * C1, 2 * Z1), BF16)),
        flops=10**9, moved=4 * 10**6,
    )
    send, back = call(
        joined_kernel, (halo,) + tuple(own) + (to_cls, to_nat, small),
        (((C3, WIDTH), BF16), ((3 * C2, L2), BF16)),
        (pltpu.VMEM((4 * C3, L3), BF16), pltpu.VMEM((C3, HALF), F32)),
    )
    got = lax.all_to_all(send.reshape(count, C3 // count, WIDTH), SPACE, 0, 0, tiled=True)
    (result,) = call(
        activation_kernel, (back, f1, weight_two, jnp.asarray(spread_matrix(), BF16)),
        (((X1L, C1, Y1 * Z1), BF16),),
        (pltpu.VMEM((9 * C2, (Y2 + 1) * Z1), BF16), pltpu.VMEM((12 * C2, 2 * Z2), BF16), pltpu.VMEM((2, 6 * C2, 4 * C1), F32)),
        flops=2 * 10**9, moved=6 * 10**6,
    )
    got = from_all("y", added(from_all("zh", added(got))))
    two, three = call(last_kernel, (got,), (((4, 27 * C1), F32), ((8, 27 * C2), F32)), limit=4)
    return result.transpose(1, 0, 2).reshape(feature_one.shape), two, three


SPACE = ("zl", "x", "core")


def solution(mesh):
    samples = mesh.shape["sample"]
    inner = 8 if samples % 8 == 0 else 1
    fine = Mesh(mesh.devices.reshape(samples // inner, inner, 2, 4, 2), ("zh", "y") + SPACE)
    brick = P(("zh", "y"), None, SPACE, None)
    return jax.shard_map(
        local,
        mesh=fine,
        in_specs=(brick, brick, brick, P(), P()),
        out_specs=(brick, P(SPACE, None), P(SPACE, None)),
        check_vma=False,
    )
```

```python
import jax
import jax.numpy as jnp
import numpy as np
from jax import lax
from jax.experimental import pallas as pl
from jax.experimental.pallas import tpu as pltpu
from jax.sharding import Mesh
from jax.sharding import PartitionSpec as P

F32, BF16 = jnp.float32, jnp.bfloat16
SLOPE = 0.3
X1L, Y1, Z1 = 4, 16, 128
Y2, Z2 = 8, 64
Y3, Z3 = 4, 32
C1, C2, C3 = 32, 64, 128
L2, L3 = Y2 * Z2, Y3 * Z3
HALF = 27 * C1 // 2
WIDTH = 27 * C2 + HALF + 16
CUBES = 32
TAP = {1: (0, 0), 2: (1, 0), 0: (1, 1)}


def class_matrix():
    m = np.zeros((L2, L2), np.float32)
    for y in range(Y2):
        for z in range(Z2):
            m[y * Z2 + z, ((y % 2) * 2 + z % 2) * L3 + (y // 2) * Z3 + z // 2] = 1
    return m


def shift_matrices():
    down = np.zeros((3, L3, L3), np.float32)
    for j in range(Y3):
        for k in range(Z3):
            for n, (dj, dk) in enumerate(((0, 1), (1, 0), (1, 1))):
                if j >= dj and k >= dk:
                    down[n, (j - dj) * Z3 + k - dk, j * Z3 + k] = 1
    up = down.transpose(0, 2, 1)
    return np.concatenate(list(down), 1), np.concatenate(list(up), 1)


def spread_matrix():
    m = np.zeros((2, Z2, 2, 3, Z1), np.float32)
    for h in range(2):
        for c in range(3):
            for k in range(Z2):
                z = 2 * k + c - 1
                if 0 <= z < Z1:
                    m[h, k, h, c, z] = 1
    return m.reshape(2 * Z2, 6 * Z1)


def pick_matrix():
    m = np.zeros((2, Z1, 3, 2, Z2), np.float32)
    for h in range(2):
        for c in range(3):
            for k in range(Z2):
                z = 2 * k + c - 1
                if 0 <= z < Z1:
                    m[h, z, c, h, k] = 1
    return m.reshape(2 * Z1, 6 * Z2)


def dot(a, b):
    return jnp.dot(a, b, preferred_element_type=F32)


def dot_nt(a, b):
    return lax.dot_general(a, b, (((1,), (1,)), ((), ())), preferred_element_type=F32)


def slope(v):
    return jnp.where(v.astype(F32) > 0, 1.0, SLOPE)


def prepare_kernel(cot, f2, layer, f2_rows, held, sems):
    copies = [
        pltpu.make_async_copy(f2, held, sems.at[0]),
        pltpu.make_async_copy(cot.at[:C2], layer.at[:, L2:L2 + L3], sems.at[1]),
        pltpu.make_async_copy(cot.at[C2:], layer.at[:, L2 + L3:], sems.at[2]),
    ]
    for copy in copies:
        copy.start()
    copies[0].wait()
    top = held[:, 0, :]
    layer[:, :L2] = top
    f2_rows[:C2, :] = top
    f2_rows[C2:, :] = held[:, 1, :]
    copies[1].wait()
    copies[2].wait()


def shifts(values, matrices, dst):
    moved = dot(values, matrices).astype(BF16)
    dst[0:C3, :] = values
    for n in range(3):
        dst[(n + 1) * C3:(n + 2) * C3, :] = moved[:, n * L3:(n + 1) * L3]


def own_kernel(cot, f2, f1, w3t, to_cls, small,
               by_tap, totals, act_cls, win_odd, we, wo, a3, cs, fw):
    down, up, pick = small[:L3, :], small[L3:2 * L3, :], small[2 * L3:, :]
    shifts(cot[...], up, cs)
    a3[...] = jnp.zeros_like(a3)
    for a in range(3):
        for b in range(3):
            for c in range(3):
                (q, f), (r, g) = TAP[b], TAP[c]
                rows, cols = (a * 4 + q * 2 + r) * C2, (f * 2 + g) * C3
                tap = (a * 9 + b * 3 + c) * C2
                a3[rows:rows + C2, cols:cols + C3] = w3t[tap:tap + C2, :]
    totals[...] = dot(a3[4 * C2:, :], cs[...])
    f2b = dot(f2[...], to_cls[...]).astype(BF16)
    act_cls[...] = f2b
    cls = [f2b[:, n * L3:(n + 1) * L3] for n in range(4)]
    moved = dot(cls[3], down).astype(BF16)
    by_k, by_j, by_jk = moved[:, :L3], moved[:, L3:2 * L3], moved[:, 2 * L3:]
    row_k = dot(cls[1], down[:, :L3]).astype(BF16)
    col_j = dot(cls[2], down[:, L3:2 * L3]).astype(BF16)
    nine = (by_jk, col_j, by_j, row_k, cls[0], cls[1], by_k, cls[2], cls[3])
    win = [jnp.concatenate([w[x * C2:(x + 1) * C2] for w in nine], axis=0) for x in range(2)]
    win_odd[...] = win[1]
    by_tap[...] = dot_nt(cot[...], jnp.concatenate(win, axis=0)).astype(BF16)
    for x in range(4):
        for b in range(3):
            for jp in range(4):
                rows = ((x * 3 + b) * 4 + jp) * C1
                y = 4 * jp + b - 1
                if y < 0:
                    fw[rows:rows + C1, :Z1] = jnp.zeros((C1, Z1), BF16)
                else:
                    fw[rows:rows + C1, :Z1] = f1[x, :, y * Z1:(y + 1) * Z1]
                fw[rows:rows + C1, Z1:] = f1[x, :, (y + 2) * Z1:(y + 3) * Z1]
    picked = dot(fw[...], pick).astype(BF16)
    for x in range(4):
        dst = (we, wo)[x % 2]
        for b in range(3):
            for jp in range(4):
                rows = ((x * 3 + b) * 4 + jp) * C1
                lane = (x // 2) * L2 + jp * 2 * Z2
                for c in range(3):
                    at = (b * 3 + c) * C1
                    dst[at:at + C1, lane:lane + 2 * Z2] = picked[rows:rows + C1, c * 2 * Z2:(c + 1) * 2 * Z2]


def joined_kernel(halo, by_tap, totals, act_cls, win_odd, we, wo, a3, to_cls, to_nat, small,
                  send, back_out, cs, g2s):
    up = small[L3:2 * L3, :]
    above = jnp.concatenate([halo[:, L2:L2 + L3], halo[:, L2 + L3:]], axis=0)
    shifts(above, up, cs)
    n4 = 4 * C2
    over = dot(a3[:2 * n4, :], cs[...])
    sums = (totals[:n4, :], totals[n4:, :] + over[:n4], over[n4:])
    above_cls = dot(halo[:, :L2], to_cls[...])
    acts = (act_cls[:C2, :], act_cls[C2:, :], above_cls)
    back_cls = []
    for x in range(3):
        tiles = []
        for n in range(4):
            gain = slope(acts[x][:, n * L3:(n + 1) * L3])
            tiles.append((sums[x][n * C2:(n + 1) * C2] * gain).astype(BF16))
        back_cls.append(jnp.concatenate(tiles, axis=1))
    back = dot(jnp.concatenate(back_cls, axis=0), to_nat[...]).astype(BF16)
    back_out[...] = back
    by_tap_above = dot_nt(above, win_odd[...])
    rows3 = [back[x * C2:(x + 1) * C2] for x in range(3)]
    pair = jnp.concatenate([jnp.concatenate([rows3[0], rows3[1]], 1), jnp.concatenate([rows3[1], rows3[2]], 1)], 0)
    even = dot_nt(pair[:C2], we[...])
    odd = dot_nt(pair, wo[...])
    grad = jnp.concatenate([odd[C2:], even, odd[:C2]], axis=1)
    first, second = grad[:, :HALF], grad[:, HALF:]
    for s in range(C2 // 4):
        g2s[8 * s:8 * s + 4, :] = first[4 * s:4 * s + 4]
        g2s[8 * s + 4:8 * s + 8, :] = second[4 * s:4 * s + 4]
    send[:, :18 * C2] = by_tap[...]
    send[:, 18 * C2:] = jnp.concatenate(
        [by_tap_above, g2s[...], jnp.zeros((C3, WIDTH - 27 * C2 - HALF), F32)], axis=1
    ).astype(BF16)


def activation_kernel(back, f1, w2, spread, out, bu, bk4, w2x):
    rows3 = [back[x * C2:(x + 1) * C2, :] for x in range(3)]
    w2x[...] = jnp.zeros_like(w2x)
    for a in range(3):
        for b in range(3):
            for c in range(3):
                (p, d), (q, f) = TAP[a], TAP[b]
                rows, cols = (d * 3 + c) * C2, (p * 2 + q) * C1
                tap = (a * 9 + b * 3 + c) * C1
                w2x[f, rows:rows + C2, cols:cols + C1] = w2[:, tap:tap + C1].astype(F32)
    w2b = [w2x[f].T.astype(BF16) for f in range(2)]
    for x in range(3):
        for jp in range(4):
            rows = (x * 4 + jp) * C2
            bk4[rows:rows + C2, :] = rows3[x][:, jp * 2 * Z2:(jp + 1) * 2 * Z2]
    wide = dot(bk4[...], spread[...]).astype(BF16)
    bu[:, Y2 * Z1:] = jnp.zeros((9 * C2, Z1), BF16)
    for x in range(3):
        for jp in range(4):
            for h in range(2):
                for c in range(3):
                    rows, at = (x * 4 + jp) * C2, (x * 3 + c) * C2
                    lane, col = (2 * jp + h) * Z1, (h * 3 + c) * Z1
                    bu[at:at + C2, lane:lane + Z1] = wide[rows:rows + C2, col:col + Z1]
    for i in range(2):
        ks = slice(i * 3 * C2, (i + 2) * 3 * C2)
        total = dot(w2b[0], bu[ks, :Y2 * Z1]) + dot(w2b[1], bu[ks, Z1:])
        for p in range(2):
            for q in range(2):
                for j in range(Y2):
                    lanes = pl.ds((2 * j + q) * Z1, Z1)
                    v = total[(p * 2 + q) * C1:(p * 2 + q + 1) * C1, j * Z1:(j + 1) * Z1]
                    out[2 * i + p, :, lanes] = (v * slope(f1[2 * i + p, :, lanes])).astype(BF16)


VM = pl.BlockSpec(memory_space=pltpu.VMEM)


def call(body, args, outs, scratch=(), flops=10**8, moved=10**6, limit=24, source=VM):
    return pl.pallas_call(
        body,
        out_shape=tuple(jax.ShapeDtypeStruct(shape, dtype) for shape, dtype in outs),
        in_specs=[source] * len(args),
        out_specs=(VM,) * len(outs),
        scratch_shapes=list(scratch),
        compiler_params=pltpu.CompilerParams(vmem_limit_bytes=limit * 1024 * 1024),
        cost_estimate=pl.CostEstimate(flops=flops, bytes_accessed=moved, transcendentals=0),
    )(*args)


def last_kernel(got, two, three):
    total = got[0].astype(F32)
    for n in range(1, got.shape[0]):
        total = total + got[n].astype(F32)
    total = total * (1.0 / CUBES)
    three[:, 9 * C2:] = total[:, :18 * C2]
    three[:, :9 * C2] = total[:, 18 * C2:27 * C2]
    two[...] = jnp.concatenate([total[:4, 27 * C2:27 * C2 + HALF], total[4:, 27 * C2:27 * C2 + HALF]], axis=1)


def added(blocks):
    total = blocks[0].astype(F32)
    for n in range(1, blocks.shape[0]):
        total = total + blocks[n].astype(F32)
    return lax.optimization_barrier(total)


def from_all(axis, part):
    count = lax.axis_size(axis)
    copies = jnp.broadcast_to(part.astype(BF16)[None], (count,) + part.shape)
    return lax.all_to_all(copies, axis, 0, 0, tiled=True)


def local(feature_one, feature_two, cotangent_three, weight_two, weight_three):
    count = lax.axis_size(SPACE)
    cls = class_matrix()
    to_cls, to_nat = jnp.asarray(cls, BF16), jnp.asarray(cls.T, BF16)
    small = jnp.asarray(np.concatenate(shift_matrices() + (pick_matrix(),), 0), BF16)
    cot = cotangent_three.reshape(C3, L3)
    layer, f2 = call(
        prepare_kernel, (cot, feature_two.reshape(C2, 2, L2)),
        (((C2, L2 + 2 * L3), BF16), ((2 * C2, L2), BF16)), (pltpu.VMEM((C2, 2, L2), BF16), pltpu.SemaphoreType.DMA((3,))),
        limit=4, source=pl.BlockSpec(memory_space=pltpu.HBM),
    )
    halo = lax.ppermute(layer, SPACE, [(n, n - 1) for n in range(1, count)])
    f1 = feature_one.reshape(C1, X1L, Y1 * Z1).transpose(1, 0, 2)
    own = call(
        own_kernel, (cot, f2, f1, weight_three.T, to_cls, small),
        (((C3, 18 * C2), BF16), ((8 * C2, L3), F32), ((2 * C2, L2), BF16), ((9 * C2, L3), BF16),
         ((9 * C1, 2 * L2), BF16), ((9 * C1, 2 * L2), BF16), ((12 * C2, 4 * C3), BF16)),
        (pltpu.VMEM((4 * C3, L3), BF16), pltpu.VMEM((48 * C1, 2 * Z1), BF16)),
        flops=10**9, moved=4 * 10**6,
    )
    send, back = call(
        joined_kernel, (halo,) + tuple(own) + (to_cls, to_nat, small),
        (((C3, WIDTH), BF16), ((3 * C2, L2), BF16)),
        (pltpu.VMEM((4 * C3, L3), BF16), pltpu.VMEM((C3, HALF), F32)),
    )
    got = lax.all_to_all(send.reshape(count, C3 // count, WIDTH), SPACE, 0, 0, tiled=True)
    (result,) = call(
        activation_kernel, (back, f1, weight_two, jnp.asarray(spread_matrix(), BF16)),
        (((X1L, C1, Y1 * Z1), BF16),),
        (pltpu.VMEM((9 * C2, (Y2 + 1) * Z1), BF16), pltpu.VMEM((12 * C2, 2 * Z2), BF16), pltpu.VMEM((2, 6 * C2, 4 * C1), F32)),
        flops=2 * 10**9, moved=6 * 10**6,
    )
    got = from_all("zh", added(from_all("y", added(got))))
    two, three = call(last_kernel, (got,), (((4, 27 * C1), F32), ((8, 27 * C2), F32)), limit=4)
    return result.transpose(1, 0, 2).reshape(feature_one.shape), two, three


SPACE = ("zl", "x", "core")


def solution(mesh):
    samples = mesh.shape["sample"]
    inner = 8 if samples % 8 == 0 else 1
    fine = Mesh(mesh.devices.reshape(samples // inner, inner, 2, 4, 2), ("zh", "y") + SPACE)
    brick = P(("zh", "y"), None, SPACE, None)
    return jax.shard_map(
        local,
        mesh=fine,
        in_specs=(brick, brick, brick, P(), P()),
        out_specs=(brick, P(SPACE, None), P(SPACE, None)),
        check_vma=False,
    )
```

```python
import jax
import jax.numpy as jnp
import numpy as np
from jax import lax
from jax.experimental import pallas as pl
from jax.experimental.pallas import tpu as pltpu
from jax.sharding import Mesh
from jax.sharding import PartitionSpec as P

F32, BF16 = jnp.float32, jnp.bfloat16
SLOPE = 0.3
X1L, Y1, Z1 = 4, 16, 128
Y2, Z2 = 8, 64
Y3, Z3 = 4, 32
C1, C2, C3 = 32, 64, 128
L2, L3 = Y2 * Z2, Y3 * Z3
HALF = 27 * C1 // 2
WIDTH = 27 * C2 + HALF + 16
CUBES = 32
TAP = {1: (0, 0), 2: (1, 0), 0: (1, 1)}


def class_matrix():
    m = np.zeros((L2, L2), np.float32)
    for y in range(Y2):
        for z in range(Z2):
            m[y * Z2 + z, ((y % 2) * 2 + z % 2) * L3 + (y // 2) * Z3 + z // 2] = 1
    return m


def shift_matrices():
    down = np.zeros((3, L3, L3), np.float32)
    for j in range(Y3):
        for k in range(Z3):
            for n, (dj, dk) in enumerate(((0, 1), (1, 0), (1, 1))):
                if j >= dj and k >= dk:
                    down[n, (j - dj) * Z3 + k - dk, j * Z3 + k] = 1
    up = down.transpose(0, 2, 1)
    return np.concatenate(list(down), 1), np.concatenate(list(up), 1)


def spread_matrix():
    m = np.zeros((2, Z2, 2, 3, Z1), np.float32)
    for h in range(2):
        for c in range(3):
            for k in range(Z2):
                z = 2 * k + c - 1
                if 0 <= z < Z1:
                    m[h, k, h, c, z] = 1
    return m.reshape(2 * Z2, 6 * Z1)


def pick_matrix():
    m = np.zeros((2, Z1, 3, 2, Z2), np.float32)
    for h in range(2):
        for c in range(3):
            for k in range(Z2):
                z = 2 * k + c - 1
                if 0 <= z < Z1:
                    m[h, z, c, h, k] = 1
    return m.reshape(2 * Z1, 6 * Z2)


def dot(a, b):
    return jnp.dot(a, b, preferred_element_type=F32)


def dot_nt(a, b):
    return lax.dot_general(a, b, (((1,), (1,)), ((), ())), preferred_element_type=F32)


def slope(v):
    return jnp.where(v.astype(F32) > 0, 1.0, SLOPE)


def prepare_kernel(cot, f2, layer, f2_rows, held, sems):
    copies = [
        pltpu.make_async_copy(f2, held, sems.at[0]),
        pltpu.make_async_copy(cot.at[:C2], layer.at[:, L2:L2 + L3], sems.at[1]),
        pltpu.make_async_copy(cot.at[C2:], layer.at[:, L2 + L3:], sems.at[2]),
    ]
    for copy in copies:
        copy.start()
    copies[0].wait()
    top = held[:, 0, :]
    layer[:, :L2] = top
    f2_rows[:C2, :] = top
    f2_rows[C2:, :] = held[:, 1, :]
    copies[1].wait()
    copies[2].wait()


def shifts(values, matrices, dst):
    moved = dot(values, matrices).astype(BF16)
    dst[0:C3, :] = values
    for n in range(3):
        dst[(n + 1) * C3:(n + 2) * C3, :] = moved[:, n * L3:(n + 1) * L3]


def own_kernel(cot, f2, f1, w3t, to_cls, small,
               by_tap, totals, act_cls, win_odd, we, wo, a3, cs, fw):
    down, up, pick = small[:L3, :], small[L3:2 * L3, :], small[2 * L3:, :]
    shifts(cot[...], up, cs)
    a3[...] = jnp.zeros_like(a3)
    for a in range(3):
        for b in range(3):
            for c in range(3):
                (q, f), (r, g) = TAP[b], TAP[c]
                rows, cols = (a * 4 + q * 2 + r) * C2, (f * 2 + g) * C3
                tap = (a * 9 + b * 3 + c) * C2
                a3[rows:rows + C2, cols:cols + C3] = w3t[tap:tap + C2, :]
    totals[...] = dot(a3[4 * C2:, :], cs[...])
    f2b = dot(f2[...], to_cls[...]).astype(BF16)
    act_cls[...] = f2b
    cls = [f2b[:, n * L3:(n + 1) * L3] for n in range(4)]
    moved = dot(cls[3], down).astype(BF16)
    by_k, by_j, by_jk = moved[:, :L3], moved[:, L3:2 * L3], moved[:, 2 * L3:]
    row_k = dot(cls[1], down[:, :L3]).astype(BF16)
    col_j = dot(cls[2], down[:, L3:2 * L3]).astype(BF16)
    nine = (by_jk, col_j, by_j, row_k, cls[0], cls[1], by_k, cls[2], cls[3])
    win = [jnp.concatenate([w[x * C2:(x + 1) * C2] for w in nine], axis=0) for x in range(2)]
    win_odd[...] = win[1]
    by_tap[...] = dot_nt(cot[...], jnp.concatenate(win, axis=0))
    for x in range(4):
        for b in range(3):
            for jp in range(4):
                rows = ((x * 3 + b) * 4 + jp) * C1
                y = 4 * jp + b - 1
                if y < 0:
                    fw[rows:rows + C1, :Z1] = jnp.zeros((C1, Z1), BF16)
                else:
                    fw[rows:rows + C1, :Z1] = f1[x, :, y * Z1:(y + 1) * Z1]
                fw[rows:rows + C1, Z1:] = f1[x, :, (y + 2) * Z1:(y + 3) * Z1]
    picked = dot(fw[...], pick).astype(BF16)
    for x in range(4):
        dst = (we, wo)[x % 2]
        for b in range(3):
            for jp in range(4):
                rows = ((x * 3 + b) * 4 + jp) * C1
                lane = (x // 2) * L2 + jp * 2 * Z2
                for c in range(3):
                    at = (b * 3 + c) * C1
                    dst[at:at + C1, lane:lane + 2 * Z2] = picked[rows:rows + C1, c * 2 * Z2:(c + 1) * 2 * Z2]


def joined_kernel(halo, by_tap, totals, act_cls, win_odd, we, wo, a3, to_cls, to_nat, small,
                  mine, other, back_out, cs, g2s):
    up = small[L3:2 * L3, :]
    above = jnp.concatenate([halo[:, L2:L2 + L3], halo[:, L2 + L3:]], axis=0)
    shifts(above, up, cs)
    n4 = 4 * C2
    over = dot(a3[:2 * n4, :], cs[...])
    sums = (totals[:n4, :], totals[n4:, :] + over[:n4], over[n4:])
    above_cls = dot(halo[:, :L2], to_cls[...])
    acts = (act_cls[:C2, :], act_cls[C2:, :], above_cls)
    back_cls = []
    for x in range(3):
        tiles = []
        for n in range(4):
            gain = slope(acts[x][:, n * L3:(n + 1) * L3])
            tiles.append((sums[x][n * C2:(n + 1) * C2] * gain).astype(BF16))
        back_cls.append(jnp.concatenate(tiles, axis=1))
    back = dot(jnp.concatenate(back_cls, axis=0), to_nat[...]).astype(BF16)
    back_out[...] = back
    by_tap_above = dot_nt(above, win_odd[...])
    rows3 = [back[x * C2:(x + 1) * C2] for x in range(3)]
    pair = jnp.concatenate([jnp.concatenate([rows3[0], rows3[1]], 1), jnp.concatenate([rows3[1], rows3[2]], 1)], 0)
    even = dot_nt(pair[:C2], we[...])
    odd = dot_nt(pair, wo[...])
    grad = jnp.concatenate([odd[C2:], even, odd[:C2]], axis=1)
    first, second = grad[:, :HALF], grad[:, HALF:]
    for s in range(C2 // 4):
        g2s[8 * s:8 * s + 4, :] = first[4 * s:4 * s + 4]
        g2s[8 * s + 4:8 * s + 8, :] = second[4 * s:4 * s + 4]
    rows = jnp.concatenate(
        [by_tap[...], by_tap_above, g2s[...], jnp.zeros((C3, WIDTH - 27 * C2 - HALF), F32)], axis=1
    ).reshape(C3 // 16, 2, 8, WIDTH)
    even_core = lax.axis_index("core") == 0
    low, high = rows[:, 0].reshape(C3 // 2, WIDTH), rows[:, 1].reshape(C3 // 2, WIDTH)
    mine[...] = jnp.where(even_core, low, high)
    other[...] = jnp.where(even_core, high, low).astype(BF16)


def activation_kernel(back, f1, w2, spread, out, bu, bk4, w2x):
    rows3 = [back[x * C2:(x + 1) * C2, :] for x in range(3)]
    w2x[...] = jnp.zeros_like(w2x)
    for a in range(3):
        for b in range(3):
            for c in range(3):
                (p, d), (q, f) = TAP[a], TAP[b]
                rows, cols = (d * 3 + c) * C2, (p * 2 + q) * C1
                tap = (a * 9 + b * 3 + c) * C1
                w2x[f, rows:rows + C2, cols:cols + C1] = w2[:, tap:tap + C1].astype(F32)
    w2b = [w2x[f].T.astype(BF16) for f in range(2)]
    for x in range(3):
        for jp in range(4):
            rows = (x * 4 + jp) * C2
            bk4[rows:rows + C2, :] = rows3[x][:, jp * 2 * Z2:(jp + 1) * 2 * Z2]
    wide = dot(bk4[...], spread[...]).astype(BF16)
    bu[:, Y2 * Z1:] = jnp.zeros((9 * C2, Z1), BF16)
    for x in range(3):
        for jp in range(4):
            for h in range(2):
                for c in range(3):
                    rows, at = (x * 4 + jp) * C2, (x * 3 + c) * C2
                    lane, col = (2 * jp + h) * Z1, (h * 3 + c) * Z1
                    bu[at:at + C2, lane:lane + Z1] = wide[rows:rows + C2, col:col + Z1]
    for i in range(2):
        ks = slice(i * 3 * C2, (i + 2) * 3 * C2)
        total = dot(w2b[0], bu[ks, :Y2 * Z1]) + dot(w2b[1], bu[ks, Z1:])
        for p in range(2):
            for q in range(2):
                for j in range(Y2):
                    lanes = pl.ds((2 * j + q) * Z1, Z1)
                    v = total[(p * 2 + q) * C1:(p * 2 + q + 1) * C1, j * Z1:(j + 1) * Z1]
                    out[2 * i + p, :, lanes] = (v * slope(f1[2 * i + p, :, lanes])).astype(BF16)


VM = pl.BlockSpec(memory_space=pltpu.VMEM)


def call(body, args, outs, scratch=(), flops=10**8, moved=10**6, limit=24, source=VM):
    return pl.pallas_call(
        body,
        out_shape=tuple(jax.ShapeDtypeStruct(shape, dtype) for shape, dtype in outs),
        in_specs=[source] * len(args),
        out_specs=(VM,) * len(outs),
        scratch_shapes=list(scratch),
        compiler_params=pltpu.CompilerParams(vmem_limit_bytes=limit * 1024 * 1024),
        cost_estimate=pl.CostEstimate(flops=flops, bytes_accessed=moved, transcendentals=0),
    )(*args)


def last_kernel(got, two, three):
    total = got[0].astype(F32)
    for n in range(1, got.shape[0]):
        total = total + got[n].astype(F32)
    total = total * (1.0 / CUBES)
    three[:, 9 * C2:] = total[:, :18 * C2]
    three[:, :9 * C2] = total[:, 18 * C2:27 * C2]
    two[...] = jnp.concatenate([total[:4, 27 * C2:27 * C2 + HALF], total[4:, 27 * C2:27 * C2 + HALF]], axis=1)


def added(blocks):
    total = blocks[0].astype(F32)
    for n in range(1, blocks.shape[0]):
        total = total + blocks[n].astype(F32)
    return lax.optimization_barrier(total)


def from_all(axis, part):
    count = lax.axis_size(axis)
    copies = jnp.broadcast_to(part.astype(BF16)[None], (count,) + part.shape)
    return lax.all_to_all(copies, axis, 0, 0, tiled=True)


def local(feature_one, feature_two, cotangent_three, weight_two, weight_three):
    count = lax.axis_size(SPACE)
    cls = class_matrix()
    to_cls, to_nat = jnp.asarray(cls, BF16), jnp.asarray(cls.T, BF16)
    small = jnp.asarray(np.concatenate(shift_matrices() + (pick_matrix(),), 0), BF16)
    cot = cotangent_three.reshape(C3, L3)
    layer, f2 = call(
        prepare_kernel, (cot, feature_two.reshape(C2, 2, L2)),
        (((C2, L2 + 2 * L3), BF16), ((2 * C2, L2), BF16)), (pltpu.VMEM((C2, 2, L2), BF16), pltpu.SemaphoreType.DMA((3,))),
        limit=60, source=pl.BlockSpec(memory_space=pltpu.HBM),
    )
    halo = lax.ppermute(layer, SPACE, [(n, n - 1) for n in range(1, count)])
    f1 = feature_one.reshape(C1, X1L, Y1 * Z1).transpose(1, 0, 2)
    own = call(
        own_kernel, (cot, f2, f1, weight_three.T, to_cls, small),
        (((C3, 18 * C2), F32), ((8 * C2, L3), F32), ((2 * C2, L2), BF16), ((9 * C2, L3), BF16),
         ((9 * C1, 2 * L2), BF16), ((9 * C1, 2 * L2), BF16), ((12 * C2, 4 * C3), BF16)),
        (pltpu.VMEM((4 * C3, L3), BF16), pltpu.VMEM((48 * C1, 2 * Z1), BF16)),
        flops=10**9, moved=4 * 10**6,
    )
    mine, other, back = call(
        joined_kernel, (halo,) + tuple(own) + (to_cls, to_nat, small),
        (((C3 // 2, WIDTH), F32), ((C3 // 2, WIDTH), BF16), ((3 * C2, L2), BF16)),
        (pltpu.VMEM((4 * C3, L3), BF16), pltpu.VMEM((C3, HALF), F32)),
    )
    both = mine + lax.ppermute(other, "core", [(0, 1), (1, 0)]).astype(F32)
    got = lax.all_to_all(both.astype(BF16).reshape(count // 2, 8, WIDTH), SPACE[:2], 0, 0, tiled=True)
    (result,) = call(
        activation_kernel, (back, f1, weight_two, jnp.asarray(spread_matrix(), BF16)),
        (((X1L, C1, Y1 * Z1), BF16),),
        (pltpu.VMEM((9 * C2, (Y2 + 1) * Z1), BF16), pltpu.VMEM((12 * C2, 2 * Z2), BF16), pltpu.VMEM((2, 6 * C2, 4 * C1), F32)),
        flops=2 * 10**9, moved=6 * 10**6,
    )
    got = from_all("y", added(from_all("zh", added(got))))
    two, three = call(last_kernel, (got,), (((4, 27 * C1), F32), ((8, 27 * C2), F32)), limit=4)
    return result.transpose(1, 0, 2).reshape(feature_one.shape), two, three


SPACE = ("zl", "x", "core")


def solution(mesh):
    samples = mesh.shape["sample"]
    inner = 8 if samples % 8 == 0 else 1
    fine = Mesh(mesh.devices.reshape(samples // inner, inner, 2, 4, 2), ("zh", "y") + SPACE)
    brick = P(("zh", "y"), None, SPACE, None)
    return jax.shard_map(
        local,
        mesh=fine,
        in_specs=(brick, brick, brick, P(), P()),
        out_specs=(brick, P(SPACE, None), P(SPACE, None)),
        check_vma=False,
    )
```

```python
import jax
import jax.numpy as jnp
import numpy as np
from jax import lax
from jax.experimental import pallas as pl
from jax.experimental.pallas import tpu as pltpu
from jax.sharding import Mesh
from jax.sharding import PartitionSpec as P

F32, BF16 = jnp.float32, jnp.bfloat16
SLOPE = 0.3
X1L, Y1, Z1 = 4, 16, 128
Y2, Z2 = 8, 64
Y3, Z3 = 4, 32
C1, C2, C3 = 32, 64, 128
L2, L3 = Y2 * Z2, Y3 * Z3
HALF = 27 * C1 // 2
WIDTH = 27 * C2 + HALF + 16
CUBES = 32
TAP = {1: (0, 0), 2: (1, 0), 0: (1, 1)}


def class_matrix():
    m = np.zeros((L2, L2), np.float32)
    for y in range(Y2):
        for z in range(Z2):
            m[y * Z2 + z, ((y % 2) * 2 + z % 2) * L3 + (y // 2) * Z3 + z // 2] = 1
    return m


def shift_matrices():
    down = np.zeros((3, L3, L3), np.float32)
    for j in range(Y3):
        for k in range(Z3):
            for n, (dj, dk) in enumerate(((0, 1), (1, 0), (1, 1))):
                if j >= dj and k >= dk:
                    down[n, (j - dj) * Z3 + k - dk, j * Z3 + k] = 1
    up = down.transpose(0, 2, 1)
    return np.concatenate(list(down), 1), np.concatenate(list(up), 1)


def spread_matrix():
    m = np.zeros((2, Z2, 2, 3, Z1), np.float32)
    for h in range(2):
        for c in range(3):
            for k in range(Z2):
                z = 2 * k + c - 1
                if 0 <= z < Z1:
                    m[h, k, h, c, z] = 1
    return m.reshape(2 * Z2, 6 * Z1)


def pick_matrix():
    m = np.zeros((2, Z1, 3, 2, Z2), np.float32)
    for h in range(2):
        for c in range(3):
            for k in range(Z2):
                z = 2 * k + c - 1
                if 0 <= z < Z1:
                    m[h, z, c, h, k] = 1
    return m.reshape(2 * Z1, 6 * Z2)


def dot(a, b):
    return jnp.dot(a, b, preferred_element_type=F32)


def dot_nt(a, b):
    return lax.dot_general(a, b, (((1,), (1,)), ((), ())), preferred_element_type=F32)


def slope(v):
    return jnp.where(v.astype(F32) > 0, 1.0, SLOPE)


def prepare_kernel(cot, f2, _, layer, f2_rows):
    top = f2[:, 0, :]
    layer[:, :L2] = top
    layer[:, L2:L2 + L3] = cot[:C2, :]
    layer[:, L2 + L3:] = cot[C2:, :]
    f2_rows[:C2, :] = top
    f2_rows[C2:, :] = f2[:, 1, :]


def shifts(values, matrices, dst):
    moved = dot(values, matrices).astype(BF16)
    dst[0:C3, :] = values
    for n in range(3):
        dst[(n + 1) * C3:(n + 2) * C3, :] = moved[:, n * L3:(n + 1) * L3]


def own_kernel(cot, f2, f1, w3t, to_cls, small,
               by_tap, totals, act_cls, win_odd, we, wo, a3, cs, fw):
    down, up, pick = small[:L3, :], small[L3:2 * L3, :], small[2 * L3:, :]
    shifts(cot[...], up, cs)
    a3[...] = jnp.zeros_like(a3)
    for a in range(3):
        for b in range(3):
            for c in range(3):
                (q, f), (r, g) = TAP[b], TAP[c]
                rows, cols = (a * 4 + q * 2 + r) * C2, (f * 2 + g) * C3
                tap = (a * 9 + b * 3 + c) * C2
                a3[rows:rows + C2, cols:cols + C3] = w3t[tap:tap + C2, :]
    totals[...] = dot(a3[4 * C2:, :], cs[...])
    f2b = dot(f2[...], to_cls[...]).astype(BF16)
    act_cls[...] = f2b
    cls = [f2b[:, n * L3:(n + 1) * L3] for n in range(4)]
    moved = dot(cls[3], down).astype(BF16)
    by_k, by_j, by_jk = moved[:, :L3], moved[:, L3:2 * L3], moved[:, 2 * L3:]
    row_k = dot(cls[1], down[:, :L3]).astype(BF16)
    col_j = dot(cls[2], down[:, L3:2 * L3]).astype(BF16)
    nine = (by_jk, col_j, by_j, row_k, cls[0], cls[1], by_k, cls[2], cls[3])
    win = [jnp.concatenate([w[x * C2:(x + 1) * C2] for w in nine], axis=0) for x in range(2)]
    win_odd[...] = win[1]
    by_tap[...] = dot_nt(cot[...], jnp.concatenate(win, axis=0))
    for x in range(4):
        for b in range(3):
            for jp in range(4):
                rows = ((x * 3 + b) * 4 + jp) * C1
                y = 4 * jp + b - 1
                if y < 0:
                    fw[rows:rows + C1, :Z1] = jnp.zeros((C1, Z1), BF16)
                else:
                    fw[rows:rows + C1, :Z1] = f1[x, :, y * Z1:(y + 1) * Z1]
                fw[rows:rows + C1, Z1:] = f1[x, :, (y + 2) * Z1:(y + 3) * Z1]
    picked = dot(fw[...], pick).astype(BF16)
    for x in range(4):
        dst = (we, wo)[x % 2]
        for b in range(3):
            for jp in range(4):
                rows = ((x * 3 + b) * 4 + jp) * C1
                lane = (x // 2) * L2 + jp * 2 * Z2
                for c in range(3):
                    at = (b * 3 + c) * C1
                    dst[at:at + C1, lane:lane + 2 * Z2] = picked[rows:rows + C1, c * 2 * Z2:(c + 1) * 2 * Z2]


def joined_kernel(halo, by_tap, totals, act_cls, win_odd, we, wo, a3, to_cls, to_nat, small,
                  mine, other, back_out, cs, g2s):
    up = small[L3:2 * L3, :]
    above = jnp.concatenate([halo[:, L2:L2 + L3], halo[:, L2 + L3:]], axis=0)
    shifts(above, up, cs)
    n4 = 4 * C2
    over = dot(a3[:2 * n4, :], cs[...])
    sums = (totals[:n4, :], totals[n4:, :] + over[:n4], over[n4:])
    above_cls = dot(halo[:, :L2], to_cls[...])
    acts = (act_cls[:C2, :], act_cls[C2:, :], above_cls)
    back_cls = []
    for x in range(3):
        tiles = []
        for n in range(4):
            gain = slope(acts[x][:, n * L3:(n + 1) * L3])
            tiles.append((sums[x][n * C2:(n + 1) * C2] * gain).astype(BF16))
        back_cls.append(jnp.concatenate(tiles, axis=1))
    back = dot(jnp.concatenate(back_cls, axis=0), to_nat[...]).astype(BF16)
    back_out[...] = back
    by_tap_above = dot_nt(above, win_odd[...])
    rows3 = [back[x * C2:(x + 1) * C2] for x in range(3)]
    pair = jnp.concatenate([jnp.concatenate([rows3[0], rows3[1]], 1), jnp.concatenate([rows3[1], rows3[2]], 1)], 0)
    even = dot_nt(pair[:C2], we[...])
    odd = dot_nt(pair, wo[...])
    grad = jnp.concatenate([odd[C2:], even, odd[:C2]], axis=1)
    first, second = grad[:, :HALF], grad[:, HALF:]
    for s in range(C2 // 4):
        g2s[8 * s:8 * s + 4, :] = first[4 * s:4 * s + 4]
        g2s[8 * s + 4:8 * s + 8, :] = second[4 * s:4 * s + 4]
    rows = jnp.concatenate(
        [by_tap[...], by_tap_above, g2s[...], jnp.zeros((C3, WIDTH - 27 * C2 - HALF), F32)], axis=1
    ).reshape(C3 // 16, 2, 8, WIDTH)
    even_core = lax.axis_index("core") == 0
    low, high = rows[:, 0].reshape(C3 // 2, WIDTH), rows[:, 1].reshape(C3 // 2, WIDTH)
    mine[...] = jnp.where(even_core, low, high)
    other[...] = jnp.where(even_core, high, low).astype(BF16)


def activation_kernel(back, f1, w2, spread, out, bu, bk4, w2x):
    rows3 = [back[x * C2:(x + 1) * C2, :] for x in range(3)]
    w2x[...] = jnp.zeros_like(w2x)
    for a in range(3):
        for b in range(3):
            for c in range(3):
                (p, d), (q, f) = TAP[a], TAP[b]
                rows, cols = (d * 3 + c) * C2, (p * 2 + q) * C1
                tap = (a * 9 + b * 3 + c) * C1
                w2x[f, rows:rows + C2, cols:cols + C1] = w2[:, tap:tap + C1].astype(F32)
    w2b = [w2x[f].T.astype(BF16) for f in range(2)]
    for x in range(3):
        for jp in range(4):
            rows = (x * 4 + jp) * C2
            bk4[rows:rows + C2, :] = rows3[x][:, jp * 2 * Z2:(jp + 1) * 2 * Z2]
    wide = dot(bk4[...], spread[...]).astype(BF16)
    bu[:, Y2 * Z1:] = jnp.zeros((9 * C2, Z1), BF16)
    for x in range(3):
        for jp in range(4):
            for h in range(2):
                for c in range(3):
                    rows, at = (x * 4 + jp) * C2, (x * 3 + c) * C2
                    lane, col = (2 * jp + h) * Z1, (h * 3 + c) * Z1
                    bu[at:at + C2, lane:lane + Z1] = wide[rows:rows + C2, col:col + Z1]
    for i in range(2):
        ks = slice(i * 3 * C2, (i + 2) * 3 * C2)
        total = dot(w2b[0], bu[ks, :Y2 * Z1]) + dot(w2b[1], bu[ks, Z1:])
        for p in range(2):
            for q in range(2):
                for j in range(Y2):
                    lanes = pl.ds((2 * j + q) * Z1, Z1)
                    v = total[(p * 2 + q) * C1:(p * 2 + q + 1) * C1, j * Z1:(j + 1) * Z1]
                    out[2 * i + p, :, lanes] = (v * slope(f1[2 * i + p, :, lanes])).astype(BF16)


VM = pl.BlockSpec(memory_space=pltpu.VMEM)


def call(body, args, outs, scratch=(), flops=10**8, moved=10**6, limit=24):
    return pl.pallas_call(
        body,
        out_shape=tuple(jax.ShapeDtypeStruct(shape, dtype) for shape, dtype in outs),
        in_specs=[VM] * len(args),
        out_specs=(VM,) * len(outs),
        scratch_shapes=list(scratch),
        compiler_params=pltpu.CompilerParams(vmem_limit_bytes=limit * 1024 * 1024),
        cost_estimate=pl.CostEstimate(flops=flops, bytes_accessed=moved, transcendentals=0),
    )(*args)


def last_kernel(got, two, three):
    total = got[0].astype(F32)
    for n in range(1, got.shape[0]):
        total = total + got[n].astype(F32)
    total = total * (1.0 / CUBES)
    three[:, 9 * C2:] = total[:, :18 * C2]
    three[:, :9 * C2] = total[:, 18 * C2:27 * C2]
    two[...] = jnp.concatenate([total[:4, 27 * C2:27 * C2 + HALF], total[4:, 27 * C2:27 * C2 + HALF]], axis=1)


def added(blocks):
    total = blocks[0].astype(F32)
    for n in range(1, blocks.shape[0]):
        total = total + blocks[n].astype(F32)
    return lax.optimization_barrier(total)


def from_all(axis, part):
    count = lax.axis_size(axis)
    copies = jnp.broadcast_to(part.astype(BF16)[None], (count,) + part.shape)
    return lax.all_to_all(copies, axis, 0, 0, tiled=True)


def local(feature_one, feature_two, cotangent_three, weight_two, weight_three):
    count = lax.axis_size(SPACE)
    cls = class_matrix()
    to_cls, to_nat = jnp.asarray(cls, BF16), jnp.asarray(cls.T, BF16)
    small = jnp.asarray(np.concatenate(shift_matrices() + (pick_matrix(),), 0), BF16)
    cot = cotangent_three.reshape(C3, L3)
    f1 = feature_one.reshape(C1, X1L, Y1 * Z1).transpose(1, 0, 2)
    layer, f2 = call(
        prepare_kernel, (cot, feature_two.reshape(C2, 2, L2), f1),
        (((C2, L2 + 2 * L3), BF16), ((2 * C2, L2), BF16)), limit=4,
    )
    halo = lax.ppermute(layer, SPACE, [(n, n - 1) for n in range(1, count)])
    own = call(
        own_kernel, (cot, f2, f1, weight_three.T, to_cls, small),
        (((C3, 18 * C2), F32), ((8 * C2, L3), F32), ((2 * C2, L2), BF16), ((9 * C2, L3), BF16),
         ((9 * C1, 2 * L2), BF16), ((9 * C1, 2 * L2), BF16), ((12 * C2, 4 * C3), BF16)),
        (pltpu.VMEM((4 * C3, L3), BF16), pltpu.VMEM((48 * C1, 2 * Z1), BF16)),
        flops=10**9, moved=4 * 10**6,
    )
    mine, other, back = call(
        joined_kernel, (halo,) + tuple(own) + (to_cls, to_nat, small),
        (((C3 // 2, WIDTH), F32), ((C3 // 2, WIDTH), BF16), ((3 * C2, L2), BF16)),
        (pltpu.VMEM((4 * C3, L3), BF16), pltpu.VMEM((C3, HALF), F32)),
    )
    both = mine + lax.ppermute(other, "core", [(0, 1), (1, 0)]).astype(F32)
    got = lax.all_to_all(both.astype(BF16).reshape(count // 2, 8, WIDTH), SPACE[:2], 0, 0, tiled=True)
    (result,) = call(
        activation_kernel, (back, f1, weight_two, jnp.asarray(spread_matrix(), BF16)),
        (((X1L, C1, Y1 * Z1), BF16),),
        (pltpu.VMEM((9 * C2, (Y2 + 1) * Z1), BF16), pltpu.VMEM((12 * C2, 2 * Z2), BF16), pltpu.VMEM((2, 6 * C2, 4 * C1), F32)),
        flops=2 * 10**9, moved=6 * 10**6,
    )
    got = from_all("y", added(from_all("zh", added(got))))
    two, three = call(last_kernel, (got,), (((4, 27 * C1), F32), ((8, 27 * C2), F32)), limit=4)
    return result.transpose(1, 0, 2).reshape(feature_one.shape), two, three


SPACE = ("zl", "x", "core")


def solution(mesh):
    samples = mesh.shape["sample"]
    inner = 8 if samples % 8 == 0 else 1
    fine = Mesh(mesh.devices.reshape(samples // inner, inner, 2, 4, 2), ("zh", "y") + SPACE)
    brick = P(("zh", "y"), None, SPACE, None)
    return jax.shard_map(
        local,
        mesh=fine,
        in_specs=(brick, brick, brick, P(), P()),
        out_specs=(brick, P(SPACE, None), P(SPACE, None)),
        check_vma=False,
    )
```

```python
import jax
import jax.numpy as jnp
import numpy as np
from jax import lax
from jax.experimental import pallas as pl
from jax.experimental.pallas import tpu as pltpu
from jax.sharding import Mesh
from jax.sharding import PartitionSpec as P

F32, BF16 = jnp.float32, jnp.bfloat16
SLOPE = 0.3
X1L, Y1, Z1 = 4, 16, 128
Y2, Z2 = 8, 64
Y3, Z3 = 4, 32
C1, C2, C3 = 32, 64, 128
L2, L3 = Y2 * Z2, Y3 * Z3
HALF = 27 * C1 // 2
WIDTH = 27 * C2 + HALF + 16
CUBES = 32
TAP = {1: (0, 0), 2: (1, 0), 0: (1, 1)}


def class_matrix():
    m = np.zeros((L2, L2), np.float32)
    for y in range(Y2):
        for z in range(Z2):
            m[y * Z2 + z, ((y % 2) * 2 + z % 2) * L3 + (y // 2) * Z3 + z // 2] = 1
    return m


def shift_matrices():
    down = np.zeros((3, L3, L3), np.float32)
    for j in range(Y3):
        for k in range(Z3):
            for n, (dj, dk) in enumerate(((0, 1), (1, 0), (1, 1))):
                if j >= dj and k >= dk:
                    down[n, (j - dj) * Z3 + k - dk, j * Z3 + k] = 1
    up = down.transpose(0, 2, 1)
    return np.concatenate(list(down), 1), np.concatenate(list(up), 1)


def spread_matrix():
    m = np.zeros((2, Z2, 2, 3, Z1), np.float32)
    for h in range(2):
        for c in range(3):
            for k in range(Z2):
                z = 2 * k + c - 1
                if 0 <= z < Z1:
                    m[h, k, h, c, z] = 1
    return m.reshape(2 * Z2, 6 * Z1)


def pick_matrix():
    m = np.zeros((2, Z1, 3, 2, Z2), np.float32)
    for h in range(2):
        for c in range(3):
            for k in range(Z2):
                z = 2 * k + c - 1
                if 0 <= z < Z1:
                    m[h, z, c, h, k] = 1
    return m.reshape(2 * Z1, 6 * Z2)


def dot(a, b):
    return jnp.dot(a, b, preferred_element_type=F32)


def dot_nt(a, b):
    return lax.dot_general(a, b, (((1,), (1,)), ((), ())), preferred_element_type=F32)


def slope(v):
    return jnp.where(v.astype(F32) > 0, 1.0, SLOPE)


def prepare_kernel(cot, f2, _, layer, f2_rows):
    top = f2[:, 0, :]
    layer[:, :L2] = top
    layer[:, L2:L2 + L3] = cot[:C2, :]
    layer[:, L2 + L3:] = cot[C2:, :]
    f2_rows[:C2, :] = top
    f2_rows[C2:, :] = f2[:, 1, :]


def shifts(values, matrices, dst):
    moved = dot(values, matrices).astype(BF16)
    dst[0:C3, :] = values
    for n in range(3):
        dst[(n + 1) * C3:(n + 2) * C3, :] = moved[:, n * L3:(n + 1) * L3]


def own_kernel(cot, f2, f1, w3t, to_cls, small,
               by_tap, totals, act_cls, win_odd, we, wo, a3, cs, fw):
    down, up, pick = small[:L3, :], small[L3:2 * L3, :], small[2 * L3:, :]
    shifts(cot[...], up, cs)
    a3[...] = jnp.zeros_like(a3)
    for a in range(3):
        for b in range(3):
            for c in range(3):
                (q, f), (r, g) = TAP[b], TAP[c]
                rows, cols = (a * 4 + q * 2 + r) * C2, (f * 2 + g) * C3
                tap = (a * 9 + b * 3 + c) * C2
                a3[rows:rows + C2, cols:cols + C3] = w3t[tap:tap + C2, :]
    totals[...] = dot(a3[4 * C2:, :], cs[...])
    f2b = dot(f2[...], to_cls[...]).astype(BF16)
    act_cls[...] = f2b
    cls = [f2b[:, n * L3:(n + 1) * L3] for n in range(4)]
    moved = dot(cls[3], down).astype(BF16)
    by_k, by_j, by_jk = moved[:, :L3], moved[:, L3:2 * L3], moved[:, 2 * L3:]
    row_k = dot(cls[1], down[:, :L3]).astype(BF16)
    col_j = dot(cls[2], down[:, L3:2 * L3]).astype(BF16)
    nine = (by_jk, col_j, by_j, row_k, cls[0], cls[1], by_k, cls[2], cls[3])
    win = [jnp.concatenate([w[x * C2:(x + 1) * C2] for w in nine], axis=0) for x in range(2)]
    win_odd[...] = win[1]
    by_tap[...] = dot_nt(cot[...], jnp.concatenate(win, axis=0)).astype(BF16)
    for x in range(4):
        for b in range(3):
            for jp in range(4):
                rows = ((x * 3 + b) * 4 + jp) * C1
                y = 4 * jp + b - 1
                if y < 0:
                    fw[rows:rows + C1, :Z1] = jnp.zeros((C1, Z1), BF16)
                else:
                    fw[rows:rows + C1, :Z1] = f1[x, :, y * Z1:(y + 1) * Z1]
                fw[rows:rows + C1, Z1:] = f1[x, :, (y + 2) * Z1:(y + 3) * Z1]
    picked = dot(fw[...], pick).astype(BF16)
    for x in range(4):
        dst = (we, wo)[x % 2]
        for b in range(3):
            for jp in range(4):
                rows = ((x * 3 + b) * 4 + jp) * C1
                lane = (x // 2) * L2 + jp * 2 * Z2
                for c in range(3):
                    at = (b * 3 + c) * C1
                    dst[at:at + C1, lane:lane + 2 * Z2] = picked[rows:rows + C1, c * 2 * Z2:(c + 1) * 2 * Z2]


def joined_kernel(halo, by_tap, totals, act_cls, win_odd, we, wo, a3, to_cls, to_nat, small,
                  send, back_out, cs, g2s):
    up = small[L3:2 * L3, :]
    above = jnp.concatenate([halo[:, L2:L2 + L3], halo[:, L2 + L3:]], axis=0)
    shifts(above, up, cs)
    n4 = 4 * C2
    over = dot(a3[:2 * n4, :], cs[...])
    sums = (totals[:n4, :], totals[n4:, :] + over[:n4], over[n4:])
    above_cls = dot(halo[:, :L2], to_cls[...])
    acts = (act_cls[:C2, :], act_cls[C2:, :], above_cls)
    back_cls = []
    for x in range(3):
        tiles = []
        for n in range(4):
            gain = slope(acts[x][:, n * L3:(n + 1) * L3])
            tiles.append((sums[x][n * C2:(n + 1) * C2] * gain).astype(BF16))
        back_cls.append(jnp.concatenate(tiles, axis=1))
    back = dot(jnp.concatenate(back_cls, axis=0), to_nat[...]).astype(BF16)
    back_out[...] = back
    by_tap_above = dot_nt(above, win_odd[...])
    rows3 = [back[x * C2:(x + 1) * C2] for x in range(3)]
    pair = jnp.concatenate([jnp.concatenate([rows3[0], rows3[1]], 1), jnp.concatenate([rows3[1], rows3[2]], 1)], 0)
    even = dot_nt(pair[:C2], we[...])
    odd = dot_nt(pair, wo[...])
    grad = jnp.concatenate([odd[C2:], even, odd[:C2]], axis=1)
    first, second = grad[:, :HALF], grad[:, HALF:]
    for s in range(C2 // 4):
        g2s[8 * s:8 * s + 4, :] = first[4 * s:4 * s + 4]
        g2s[8 * s + 4:8 * s + 8, :] = second[4 * s:4 * s + 4]
    send[:, :18 * C2] = by_tap[...]
    send[:, 18 * C2:] = jnp.concatenate(
        [by_tap_above, g2s[...], jnp.zeros((C3, WIDTH - 27 * C2 - HALF), F32)], axis=1
    ).astype(BF16)


def activation_kernel(back, f1, w2, spread, out, bu, bk4, w2x):
    rows3 = [back[x * C2:(x + 1) * C2, :] for x in range(3)]
    w2x[...] = jnp.zeros_like(w2x)
    for a in range(3):
        for b in range(3):
            for c in range(3):
                (p, d), (q, f) = TAP[a], TAP[b]
                rows, cols = (d * 3 + c) * C2, (p * 2 + q) * C1
                tap = (a * 9 + b * 3 + c) * C1
                w2x[f, rows:rows + C2, cols:cols + C1] = w2[:, tap:tap + C1].astype(F32)
    w2b = [w2x[f].T.astype(BF16) for f in range(2)]
    for x in range(3):
        for jp in range(4):
            rows = (x * 4 + jp) * C2
            bk4[rows:rows + C2, :] = rows3[x][:, jp * 2 * Z2:(jp + 1) * 2 * Z2]
    wide = dot(bk4[...], spread[...]).astype(BF16)
    bu[:, Y2 * Z1:] = jnp.zeros((9 * C2, Z1), BF16)
    for x in range(3):
        for jp in range(4):
            for h in range(2):
                for c in range(3):
                    rows, at = (x * 4 + jp) * C2, (x * 3 + c) * C2
                    lane, col = (2 * jp + h) * Z1, (h * 3 + c) * Z1
                    bu[at:at + C2, lane:lane + Z1] = wide[rows:rows + C2, col:col + Z1]
    for i in range(2):
        ks = slice(i * 3 * C2, (i + 2) * 3 * C2)
        total = dot(w2b[0], bu[ks, :Y2 * Z1]) + dot(w2b[1], bu[ks, Z1:])
        for p in range(2):
            for q in range(2):
                for j in range(Y2):
                    lanes = pl.ds((2 * j + q) * Z1, Z1)
                    v = total[(p * 2 + q) * C1:(p * 2 + q + 1) * C1, j * Z1:(j + 1) * Z1]
                    out[2 * i + p, :, lanes] = (v * slope(f1[2 * i + p, :, lanes])).astype(BF16)


VM = pl.BlockSpec(memory_space=pltpu.VMEM)


def call(body, args, outs, scratch=(), flops=10**8, moved=10**6, limit=24):
    return pl.pallas_call(
        body,
        out_shape=tuple(jax.ShapeDtypeStruct(shape, dtype) for shape, dtype in outs),
        in_specs=[VM] * len(args),
        out_specs=(VM,) * len(outs),
        scratch_shapes=list(scratch),
        compiler_params=pltpu.CompilerParams(vmem_limit_bytes=limit * 1024 * 1024),
        cost_estimate=pl.CostEstimate(flops=flops, bytes_accessed=moved, transcendentals=0),
    )(*args)


def last_kernel(got, two, three):
    total = got[0].astype(F32)
    for n in range(1, got.shape[0]):
        total = total + got[n].astype(F32)
    total = total * (1.0 / CUBES)
    three[:, 9 * C2:] = total[:, :18 * C2]
    three[:, :9 * C2] = total[:, 18 * C2:27 * C2]
    two[...] = jnp.concatenate([total[:4, 27 * C2:27 * C2 + HALF], total[4:, 27 * C2:27 * C2 + HALF]], axis=1)


def added(blocks):
    total = blocks[0].astype(F32)
    for n in range(1, blocks.shape[0]):
        total = total + blocks[n].astype(F32)
    return lax.optimization_barrier(total)


def from_all(axis, part):
    count = lax.axis_size(axis)
    copies = jnp.broadcast_to(part.astype(BF16)[None], (count,) + part.shape)
    return lax.all_to_all(copies, axis, 0, 0, tiled=True)


def local(feature_one, feature_two, cotangent_three, weight_two, weight_three):
    count = lax.axis_size(SPACE)
    cls = class_matrix()
    to_cls, to_nat = jnp.asarray(cls, BF16), jnp.asarray(cls.T, BF16)
    small = jnp.asarray(np.concatenate(shift_matrices() + (pick_matrix(),), 0), BF16)
    cot = cotangent_three.reshape(C3, L3)
    f1 = feature_one.reshape(C1, X1L, Y1 * Z1).transpose(1, 0, 2)
    layer, f2 = call(
        prepare_kernel, (cot, feature_two.reshape(C2, 2, L2), f1),
        (((C2, L2 + 2 * L3), BF16), ((2 * C2, L2), BF16)), limit=4,
    )
    halo = lax.ppermute(layer, SPACE, [(n, n - 1) for n in range(1, count)])
    own = call(
        own_kernel, (cot, f2, f1, weight_three.T, to_cls, small),
        (((C3, 18 * C2), BF16), ((8 * C2, L3), F32), ((2 * C2, L2), BF16), ((9 * C2, L3), BF16),
         ((9 * C1, 2 * L2), BF16), ((9 * C1, 2 * L2), BF16), ((12 * C2, 4 * C3), BF16)),
        (pltpu.VMEM((4 * C3, L3), BF16), pltpu.VMEM((48 * C1, 2 * Z1), BF16)),
        flops=10**9, moved=4 * 10**6,
    )
    send, back = call(
        joined_kernel, (halo,) + tuple(own) + (to_cls, to_nat, small),
        (((C3, WIDTH), BF16), ((3 * C2, L2), BF16)),
        (pltpu.VMEM((4 * C3, L3), BF16), pltpu.VMEM((C3, HALF), F32)),
    )
    got = lax.all_to_all(send.reshape(count, C3 // count, WIDTH), SPACE, 0, 0, tiled=True)
    (result,) = call(
        activation_kernel, (back, f1, weight_two, jnp.asarray(spread_matrix(), BF16)),
        (((X1L, C1, Y1 * Z1), BF16),),
        (pltpu.VMEM((9 * C2, (Y2 + 1) * Z1), BF16), pltpu.VMEM((12 * C2, 2 * Z2), BF16), pltpu.VMEM((2, 6 * C2, 4 * C1), F32)),
        flops=2 * 10**9, moved=6 * 10**6,
    )
    got = from_all("y", added(from_all("zh", added(got))))
    two, three = call(last_kernel, (got,), (((4, 27 * C1), F32), ((8, 27 * C2), F32)), limit=4)
    return result.transpose(1, 0, 2).reshape(feature_one.shape), two, three


SPACE = ("zl", "x", "core")


def solution(mesh):
    samples = mesh.shape["sample"]
    inner = 8 if samples % 8 == 0 else 1
    fine = Mesh(mesh.devices.reshape(samples // inner, inner, 2, 4, 2), ("zh", "y") + SPACE)
    brick = P(("zh", "y"), None, SPACE, None)
    return jax.shard_map(
        local,
        mesh=fine,
        in_specs=(brick, brick, brick, P(), P()),
        out_specs=(brick, P(SPACE, None), P(SPACE, None)),
        check_vma=False,
    )
```

```python
import jax
import jax.numpy as jnp
import numpy as np
from jax import lax
from jax.experimental import pallas as pl
from jax.experimental.pallas import tpu as pltpu
from jax.sharding import Mesh
from jax.sharding import PartitionSpec as P

F32, BF16 = jnp.float32, jnp.bfloat16
SLOPE = 0.3
X1L, Y1, Z1 = 4, 16, 128
Y2, Z2 = 8, 64
Y3, Z3 = 4, 32
C1, C2, C3 = 32, 64, 128
L2, L3 = Y2 * Z2, Y3 * Z3
HALF = 27 * C1 // 2
WIDTH = 27 * C2 + HALF + 16
CUBES = 32
TAP = {1: (0, 0), 2: (1, 0), 0: (1, 1)}


def class_matrix():
    m = np.zeros((L2, L2), np.float32)
    for y in range(Y2):
        for z in range(Z2):
            m[y * Z2 + z, ((y % 2) * 2 + z % 2) * L3 + (y // 2) * Z3 + z // 2] = 1
    return m


def shift_matrices():
    down = np.zeros((3, L3, L3), np.float32)
    for j in range(Y3):
        for k in range(Z3):
            for n, (dj, dk) in enumerate(((0, 1), (1, 0), (1, 1))):
                if j >= dj and k >= dk:
                    down[n, (j - dj) * Z3 + k - dk, j * Z3 + k] = 1
    up = down.transpose(0, 2, 1)
    return np.concatenate(list(down), 1), np.concatenate(list(up), 1)


def spread_matrix():
    m = np.zeros((2, Z2, 2, 3, Z1), np.float32)
    for h in range(2):
        for c in range(3):
            for k in range(Z2):
                z = 2 * k + c - 1
                if 0 <= z < Z1:
                    m[h, k, h, c, z] = 1
    return m.reshape(2 * Z2, 6 * Z1)


def pick_matrix():
    m = np.zeros((2, Z1, 3, 2, Z2), np.float32)
    for h in range(2):
        for c in range(3):
            for k in range(Z2):
                z = 2 * k + c - 1
                if 0 <= z < Z1:
                    m[h, z, c, h, k] = 1
    return m.reshape(2 * Z1, 6 * Z2)


def dot(a, b):
    return jnp.dot(a, b, preferred_element_type=F32)


def dot_nt(a, b):
    return lax.dot_general(a, b, (((1,), (1,)), ((), ())), preferred_element_type=F32)


def slope(v):
    return jnp.where(v.astype(F32) > 0, 1.0, SLOPE)


def prepare_kernel(cot, f2, _, layer, f2_rows):
    top = f2[:, 0, :]
    layer[:, :L2] = top
    layer[:, L2:L2 + L3] = cot[:C2, :]
    layer[:, L2 + L3:] = cot[C2:, :]
    f2_rows[:C2, :] = top
    f2_rows[C2:, :] = f2[:, 1, :]


def shifts(values, matrices, dst):
    moved = dot(values, matrices).astype(BF16)
    dst[0:C3, :] = values
    for n in range(3):
        dst[(n + 1) * C3:(n + 2) * C3, :] = moved[:, n * L3:(n + 1) * L3]


def own_kernel(cot, f2, f1, w3t, to_cls, small,
               by_tap, totals, act_cls, win_odd, we, wo, a3, cs, fw):
    down, up, pick = small[:L3, :], small[L3:2 * L3, :], small[2 * L3:, :]
    shifts(cot[...], up, cs)
    a3[...] = jnp.zeros_like(a3)
    for a in range(3):
        for b in range(3):
            for c in range(3):
                (q, f), (r, g) = TAP[b], TAP[c]
                rows, cols = (a * 4 + q * 2 + r) * C2, (f * 2 + g) * C3
                tap = (a * 9 + b * 3 + c) * C2
                a3[rows:rows + C2, cols:cols + C3] = w3t[tap:tap + C2, :]
    totals[...] = dot(a3[4 * C2:, :], cs[...])
    f2b = dot(f2[...], to_cls[...]).astype(BF16)
    act_cls[...] = f2b
    cls = [f2b[:, n * L3:(n + 1) * L3] for n in range(4)]
    moved = dot(cls[3], down).astype(BF16)
    by_k, by_j, by_jk = moved[:, :L3], moved[:, L3:2 * L3], moved[:, 2 * L3:]
    row_k = dot(cls[1], down[:, :L3]).astype(BF16)
    col_j = dot(cls[2], down[:, L3:2 * L3]).astype(BF16)
    nine = (by_jk, col_j, by_j, row_k, cls[0], cls[1], by_k, cls[2], cls[3])
    win = [jnp.concatenate([w[x * C2:(x + 1) * C2] for w in nine], axis=0) for x in range(2)]
    win_odd[...] = win[1]
    by_tap[...] = dot_nt(cot[...], jnp.concatenate(win, axis=0)).astype(BF16)
    for x in range(4):
        for b in range(3):
            for jp in range(4):
                rows = ((x * 3 + b) * 4 + jp) * C1
                y = 4 * jp + b - 1
                if y < 0:
                    fw[rows:rows + C1, :Z1] = jnp.zeros((C1, Z1), BF16)
                else:
                    fw[rows:rows + C1, :Z1] = f1[x, :, y * Z1:(y + 1) * Z1]
                fw[rows:rows + C1, Z1:] = f1[x, :, (y + 2) * Z1:(y + 3) * Z1]
    picked = dot(fw[...], pick).astype(BF16)
    for x in range(4):
        dst = (we, wo)[x % 2]
        for b in range(3):
            for jp in range(4):
                rows = ((x * 3 + b) * 4 + jp) * C1
                lane = (x // 2) * L2 + jp * 2 * Z2
                for c in range(3):
                    at = (b * 3 + c) * C1
                    dst[at:at + C1, lane:lane + 2 * Z2] = picked[rows:rows + C1, c * 2 * Z2:(c + 1) * 2 * Z2]


def joined_kernel(halo, by_tap, totals, act_cls, win_odd, we, wo, a3, to_cls, to_nat, small,
                  send, back_out, cs, g2s):
    up = small[L3:2 * L3, :]
    above = jnp.concatenate([halo[:, L2:L2 + L3], halo[:, L2 + L3:]], axis=0)
    shifts(above, up, cs)
    n4 = 4 * C2
    over = dot(a3[:2 * n4, :], cs[...])
    sums = (totals[:n4, :], totals[n4:, :] + over[:n4], over[n4:])
    above_cls = dot(halo[:, :L2], to_cls[...])
    acts = (act_cls[:C2, :], act_cls[C2:, :], above_cls)
    back_cls = []
    for x in range(3):
        tiles = []
        for n in range(4):
            gain = slope(acts[x][:, n * L3:(n + 1) * L3])
            tiles.append((sums[x][n * C2:(n + 1) * C2] * gain).astype(BF16))
        back_cls.append(jnp.concatenate(tiles, axis=1))
    back = dot(jnp.concatenate(back_cls, axis=0), to_nat[...]).astype(BF16)
    back_out[...] = back
    by_tap_above = dot_nt(above, win_odd[...])
    rows3 = [back[x * C2:(x + 1) * C2] for x in range(3)]
    pair = jnp.concatenate([jnp.concatenate([rows3[0], rows3[1]], 1), jnp.concatenate([rows3[1], rows3[2]], 1)], 0)
    even = dot_nt(pair[:C2], we[...])
    odd = dot_nt(pair, wo[...])
    grad = jnp.concatenate([odd[C2:], even, odd[:C2]], axis=1)
    first, second = grad[:, :HALF], grad[:, HALF:]
    for s in range(C2 // 4):
        g2s[8 * s:8 * s + 4, :] = first[4 * s:4 * s + 4]
        g2s[8 * s + 4:8 * s + 8, :] = second[4 * s:4 * s + 4]
    send[:, :18 * C2] = by_tap[...]
    send[:, 18 * C2:] = jnp.concatenate(
        [by_tap_above, g2s[...], jnp.zeros((C3, WIDTH - 27 * C2 - HALF), F32)], axis=1
    ).astype(BF16)


def activation_kernel(back, f1, w2, spread, out, bu, bk4, w2x):
    rows3 = [back[x * C2:(x + 1) * C2, :] for x in range(3)]
    w2x[...] = jnp.zeros_like(w2x)
    for a in range(3):
        for b in range(3):
            for c in range(3):
                (p, d), (q, f) = TAP[a], TAP[b]
                rows, cols = (d * 3 + c) * C2, (p * 2 + q) * C1
                tap = (a * 9 + b * 3 + c) * C1
                w2x[f, rows:rows + C2, cols:cols + C1] = w2[:, tap:tap + C1].astype(F32)
    w2b = [w2x[f].T.astype(BF16) for f in range(2)]
    for x in range(3):
        for jp in range(4):
            rows = (x * 4 + jp) * C2
            bk4[rows:rows + C2, :] = rows3[x][:, jp * 2 * Z2:(jp + 1) * 2 * Z2]
    wide = dot(bk4[...], spread[...]).astype(BF16)
    bu[:, Y2 * Z1:] = jnp.zeros((9 * C2, Z1), BF16)
    for x in range(3):
        for jp in range(4):
            for h in range(2):
                for c in range(3):
                    rows, at = (x * 4 + jp) * C2, (x * 3 + c) * C2
                    lane, col = (2 * jp + h) * Z1, (h * 3 + c) * Z1
                    bu[at:at + C2, lane:lane + Z1] = wide[rows:rows + C2, col:col + Z1]
    for i in range(2):
        ks = slice(i * 3 * C2, (i + 2) * 3 * C2)
        total = dot(w2b[0], bu[ks, :Y2 * Z1]) + dot(w2b[1], bu[ks, Z1:])
        for p in range(2):
            for q in range(2):
                for j in range(Y2):
                    lanes = pl.ds((2 * j + q) * Z1, Z1)
                    v = total[(p * 2 + q) * C1:(p * 2 + q + 1) * C1, j * Z1:(j + 1) * Z1]
                    out[2 * i + p, :, lanes] = (v * slope(f1[2 * i + p, :, lanes])).astype(BF16)


VM = pl.BlockSpec(memory_space=pltpu.VMEM)


def call(body, args, outs, scratch=(), flops=10**8, moved=10**6, limit=24):
    return pl.pallas_call(
        body,
        out_shape=tuple(jax.ShapeDtypeStruct(shape, dtype) for shape, dtype in outs),
        in_specs=[VM] * len(args),
        out_specs=(VM,) * len(outs),
        scratch_shapes=list(scratch),
        compiler_params=pltpu.CompilerParams(vmem_limit_bytes=limit * 1024 * 1024),
        cost_estimate=pl.CostEstimate(flops=flops, bytes_accessed=moved, transcendentals=0),
    )(*args)


def last_kernel(got, two, three):
    total = got[...] * (1.0 / CUBES)
    three[:, 9 * C2:] = total[:, :18 * C2]
    three[:, :9 * C2] = total[:, 18 * C2:27 * C2]
    two[...] = jnp.concatenate([total[:4, 27 * C2:27 * C2 + HALF], total[4:, 27 * C2:27 * C2 + HALF]], axis=1)


def added(blocks):
    total = blocks[0].astype(F32)
    for n in range(1, blocks.shape[0]):
        total = total + blocks[n].astype(F32)
    return lax.optimization_barrier(total)


def local(feature_one, feature_two, cotangent_three, weight_two, weight_three):
    count = lax.axis_size(SPACE)
    cls = class_matrix()
    to_cls, to_nat = jnp.asarray(cls, BF16), jnp.asarray(cls.T, BF16)
    small = jnp.asarray(np.concatenate(shift_matrices() + (pick_matrix(),), 0), BF16)
    cot = cotangent_three.reshape(C3, L3)
    f1 = feature_one.reshape(C1, X1L, Y1 * Z1).transpose(1, 0, 2)
    layer, f2 = call(
        prepare_kernel, (cot, feature_two.reshape(C2, 2, L2), f1),
        (((C2, L2 + 2 * L3), BF16), ((2 * C2, L2), BF16)), limit=4,
    )
    halo = lax.ppermute(layer, SPACE, [(n, n - 1) for n in range(1, count)])
    own = call(
        own_kernel, (cot, f2, f1, weight_three.T, to_cls, small),
        (((C3, 18 * C2), BF16), ((8 * C2, L3), F32), ((2 * C2, L2), BF16), ((9 * C2, L3), BF16),
         ((9 * C1, 2 * L2), BF16), ((9 * C1, 2 * L2), BF16), ((12 * C2, 4 * C3), BF16)),
        (pltpu.VMEM((4 * C3, L3), BF16), pltpu.VMEM((48 * C1, 2 * Z1), BF16)),
        flops=10**9, moved=4 * 10**6,
    )
    send, back = call(
        joined_kernel, (halo,) + tuple(own) + (to_cls, to_nat, small),
        (((C3, WIDTH), BF16), ((3 * C2, L2), BF16)),
        (pltpu.VMEM((4 * C3, L3), BF16), pltpu.VMEM((C3, HALF), F32)),
    )
    got = lax.all_to_all(send.reshape(count, C3 // count, WIDTH), SPACE, 0, 0, tiled=True)
    (result,) = call(
        activation_kernel, (back, f1, weight_two, jnp.asarray(spread_matrix(), BF16)),
        (((X1L, C1, Y1 * Z1), BF16),),
        (pltpu.VMEM((9 * C2, (Y2 + 1) * Z1), BF16), pltpu.VMEM((12 * C2, 2 * Z2), BF16), pltpu.VMEM((2, 6 * C2, 4 * C1), F32)),
        flops=2 * 10**9, moved=6 * 10**6,
    )
    rows, planes = lax.axis_size("y"), lax.axis_size("zh")
    part = added(got).astype(BF16).reshape(1, 8, 1, WIDTH)
    part = jnp.broadcast_to(part, (planes, 8, 1, WIDTH)).reshape(planes * 8, 1, WIDTH)
    row = added(lax.all_to_all(part, ("zh", "y"), 0, 0, tiled=True))
    got = lax.all_to_all(jnp.broadcast_to(row[None], (rows, 1, WIDTH)), "y", 0, 0, tiled=True)
    two, three = call(last_kernel, (got.reshape(8, WIDTH),), (((4, 27 * C1), F32), ((8, 27 * C2), F32)), limit=4)
    return result.transpose(1, 0, 2).reshape(feature_one.shape), two, three


SPACE = ("zl", "x", "core")


def solution(mesh):
    samples = mesh.shape["sample"]
    inner = 8 if samples % 8 == 0 else 1
    fine = Mesh(mesh.devices.reshape(samples // inner, inner, 2, 4, 2), ("zh", "y") + SPACE)
    brick = P(("zh", "y"), None, SPACE, None)
    return jax.shard_map(
        local,
        mesh=fine,
        in_specs=(brick, brick, brick, P(), P()),
        out_specs=(brick, P(SPACE, None), P(SPACE, None)),
        check_vma=False,
    )
```

```python
import jax
import jax.numpy as jnp
import numpy as np
from jax import lax
from jax.experimental import pallas as pl
from jax.experimental.pallas import tpu as pltpu
from jax.sharding import Mesh
from jax.sharding import PartitionSpec as P

F32, BF16 = jnp.float32, jnp.bfloat16
SLOPE = 0.3
X1L, Y1, Z1 = 4, 16, 128
Y2, Z2 = 8, 64
Y3, Z3 = 4, 32
C1, C2, C3 = 32, 64, 128
L2, L3 = Y2 * Z2, Y3 * Z3
HALF = 27 * C1 // 2
WIDTH = 27 * C2 + HALF + 16
CUBES = 32
TAP = {1: (0, 0), 2: (1, 0), 0: (1, 1)}


def class_matrix():
    m = np.zeros((L2, L2), np.float32)
    for y in range(Y2):
        for z in range(Z2):
            m[y * Z2 + z, ((y % 2) * 2 + z % 2) * L3 + (y // 2) * Z3 + z // 2] = 1
    return m


def shift_matrices():
    down = np.zeros((3, L3, L3), np.float32)
    for j in range(Y3):
        for k in range(Z3):
            for n, (dj, dk) in enumerate(((0, 1), (1, 0), (1, 1))):
                if j >= dj and k >= dk:
                    down[n, (j - dj) * Z3 + k - dk, j * Z3 + k] = 1
    up = down.transpose(0, 2, 1)
    return np.concatenate(list(down), 1), np.concatenate(list(up), 1)


def spread_matrix():
    m = np.zeros((2, Z2, 2, 3, Z1), np.float32)
    for h in range(2):
        for c in range(3):
            for k in range(Z2):
                z = 2 * k + c - 1
                if 0 <= z < Z1:
                    m[h, k, h, c, z] = 1
    return m.reshape(2 * Z2, 6 * Z1)


def pick_matrix():
    m = np.zeros((2, Z1, 3, 2, Z2), np.float32)
    for h in range(2):
        for c in range(3):
            for k in range(Z2):
                z = 2 * k + c - 1
                if 0 <= z < Z1:
                    m[h, z, c, h, k] = 1
    return m.reshape(2 * Z1, 6 * Z2)


def dot(a, b):
    return jnp.dot(a, b, preferred_element_type=F32)


def dot_nt(a, b):
    return lax.dot_general(a, b, (((1,), (1,)), ((), ())), preferred_element_type=F32)


def slope(v):
    return jnp.where(v.astype(F32) > 0, 1.0, SLOPE)


def prepare_kernel(cot, f2, _, layer, f2_rows):
    top = f2[:, 0, :]
    layer[:, :L2] = top
    layer[:, L2:L2 + L3] = cot[:C2, :]
    layer[:, L2 + L3:] = cot[C2:, :]
    f2_rows[:C2, :] = top
    f2_rows[C2:, :] = f2[:, 1, :]


def shifts(values, matrices, dst):
    moved = dot(values, matrices).astype(BF16)
    dst[0:C3, :] = values
    for n in range(3):
        dst[(n + 1) * C3:(n + 2) * C3, :] = moved[:, n * L3:(n + 1) * L3]


def own_kernel(cot, f2, f1, w3t, to_cls, small,
               by_tap, totals, act_cls, win_odd, we_t, wo_t, a3, cs, fw, we, wo):
    down, up, pick = small[:L3, :], small[L3:2 * L3, :], small[2 * L3:, :]
    shifts(cot[...], up, cs)
    a3[...] = jnp.zeros_like(a3)
    for a in range(3):
        for b in range(3):
            for c in range(3):
                (q, f), (r, g) = TAP[b], TAP[c]
                rows, cols = (a * 4 + q * 2 + r) * C2, (f * 2 + g) * C3
                tap = (a * 9 + b * 3 + c) * C2
                a3[rows:rows + C2, cols:cols + C3] = w3t[tap:tap + C2, :]
    totals[...] = dot(a3[4 * C2:, :], cs[...])
    f2b = dot(f2[...], to_cls[...]).astype(BF16)
    act_cls[...] = f2b
    cls = [f2b[:, n * L3:(n + 1) * L3] for n in range(4)]
    moved = dot(cls[3], down).astype(BF16)
    by_k, by_j, by_jk = moved[:, :L3], moved[:, L3:2 * L3], moved[:, 2 * L3:]
    row_k = dot(cls[1], down[:, :L3]).astype(BF16)
    col_j = dot(cls[2], down[:, L3:2 * L3]).astype(BF16)
    nine = (by_jk, col_j, by_j, row_k, cls[0], cls[1], by_k, cls[2], cls[3])
    win = [jnp.concatenate([w[x * C2:(x + 1) * C2] for w in nine], axis=0) for x in range(2)]
    win_odd[...] = win[1].T
    by_tap[...] = dot_nt(cot[...], jnp.concatenate(win, axis=0)).astype(BF16)
    for x in range(4):
        for b in range(3):
            for jp in range(4):
                rows = ((x * 3 + b) * 4 + jp) * C1
                y = 4 * jp + b - 1
                if y < 0:
                    fw[rows:rows + C1, :Z1] = jnp.zeros((C1, Z1), BF16)
                else:
                    fw[rows:rows + C1, :Z1] = f1[x, :, y * Z1:(y + 1) * Z1]
                fw[rows:rows + C1, Z1:] = f1[x, :, (y + 2) * Z1:(y + 3) * Z1]
    picked = dot(fw[...], pick).astype(BF16)
    for x in range(4):
        dst = (we, wo)[x % 2]
        for b in range(3):
            for jp in range(4):
                rows = ((x * 3 + b) * 4 + jp) * C1
                lane = (x // 2) * L2 + jp * 2 * Z2
                for c in range(3):
                    at = (b * 3 + c) * C1
                    dst[at:at + C1, lane:lane + 2 * Z2] = picked[rows:rows + C1, c * 2 * Z2:(c + 1) * 2 * Z2]
    we_t[...] = we[...].T
    wo_t[...] = wo[...].T


def joined_kernel(halo, by_tap, totals, act_cls, win_odd, we_t, wo_t, a3, to_cls, to_nat, small,
                  send, back_out, cs, g2s):
    up = small[L3:2 * L3, :]
    above = jnp.concatenate([halo[:, L2:L2 + L3], halo[:, L2 + L3:]], axis=0)
    shifts(above, up, cs)
    n4 = 4 * C2
    over = dot(a3[:2 * n4, :], cs[...])
    sums = (totals[:n4, :], totals[n4:, :] + over[:n4], over[n4:])
    above_cls = dot(halo[:, :L2], to_cls[...])
    acts = (act_cls[:C2, :], act_cls[C2:, :], above_cls)
    back_cls = []
    for x in range(3):
        tiles = []
        for n in range(4):
            gain = slope(acts[x][:, n * L3:(n + 1) * L3])
            tiles.append((sums[x][n * C2:(n + 1) * C2] * gain).astype(BF16))
        back_cls.append(jnp.concatenate(tiles, axis=1))
    back = dot(jnp.concatenate(back_cls, axis=0), to_nat[...]).astype(BF16)
    back_out[...] = back
    by_tap_above = dot(above, win_odd[...])
    rows3 = [back[x * C2:(x + 1) * C2] for x in range(3)]
    pair = jnp.concatenate([jnp.concatenate([rows3[0], rows3[1]], 1), jnp.concatenate([rows3[1], rows3[2]], 1)], 0)
    even = dot(pair[:C2], we_t[...])
    odd = dot(pair, wo_t[...])
    grad = jnp.concatenate([odd[C2:], even, odd[:C2]], axis=1)
    first, second = grad[:, :HALF], grad[:, HALF:]
    for s in range(C2 // 4):
        g2s[8 * s:8 * s + 4, :] = first[4 * s:4 * s + 4]
        g2s[8 * s + 4:8 * s + 8, :] = second[4 * s:4 * s + 4]
    send[:, :18 * C2] = by_tap[...]
    send[:, 18 * C2:] = jnp.concatenate(
        [by_tap_above, g2s[...], jnp.zeros((C3, WIDTH - 27 * C2 - HALF), F32)], axis=1
    ).astype(BF16)


def activation_kernel(back, f1, w2, spread, out, bu, bk4, w2x):
    rows3 = [back[x * C2:(x + 1) * C2, :] for x in range(3)]
    w2x[...] = jnp.zeros_like(w2x)
    for a in range(3):
        for b in range(3):
            for c in range(3):
                (p, d), (q, f) = TAP[a], TAP[b]
                rows, cols = (d * 3 + c) * C2, (p * 2 + q) * C1
                tap = (a * 9 + b * 3 + c) * C1
                w2x[f, rows:rows + C2, cols:cols + C1] = w2[:, tap:tap + C1].astype(F32)
    w2b = [w2x[f].T.astype(BF16) for f in range(2)]
    for x in range(3):
        for jp in range(4):
            rows = (x * 4 + jp) * C2
            bk4[rows:rows + C2, :] = rows3[x][:, jp * 2 * Z2:(jp + 1) * 2 * Z2]
    wide = dot(bk4[...], spread[...]).astype(BF16)
    bu[:, Y2 * Z1:] = jnp.zeros((9 * C2, Z1), BF16)
    for x in range(3):
        for jp in range(4):
            for h in range(2):
                for c in range(3):
                    rows, at = (x * 4 + jp) * C2, (x * 3 + c) * C2
                    lane, col = (2 * jp + h) * Z1, (h * 3 + c) * Z1
                    bu[at:at + C2, lane:lane + Z1] = wide[rows:rows + C2, col:col + Z1]
    for i in range(2):
        ks = slice(i * 3 * C2, (i + 2) * 3 * C2)
        total = dot(w2b[0], bu[ks, :Y2 * Z1]) + dot(w2b[1], bu[ks, Z1:])
        for p in range(2):
            for q in range(2):
                for j in range(Y2):
                    lanes = pl.ds((2 * j + q) * Z1, Z1)
                    v = total[(p * 2 + q) * C1:(p * 2 + q + 1) * C1, j * Z1:(j + 1) * Z1]
                    out[2 * i + p, :, lanes] = (v * slope(f1[2 * i + p, :, lanes])).astype(BF16)


VM = pl.BlockSpec(memory_space=pltpu.VMEM)


def call(body, args, outs, scratch=(), flops=10**8, moved=10**6, limit=24):
    return pl.pallas_call(
        body,
        out_shape=tuple(jax.ShapeDtypeStruct(shape, dtype) for shape, dtype in outs),
        in_specs=[VM] * len(args),
        out_specs=(VM,) * len(outs),
        scratch_shapes=list(scratch),
        compiler_params=pltpu.CompilerParams(vmem_limit_bytes=limit * 1024 * 1024),
        cost_estimate=pl.CostEstimate(flops=flops, bytes_accessed=moved, transcendentals=0),
    )(*args)


def last_kernel(got, two, three):
    total = got[0].astype(F32)
    for n in range(1, got.shape[0]):
        total = total + got[n].astype(F32)
    total = total * (1.0 / CUBES)
    three[:, 9 * C2:] = total[:, :18 * C2]
    three[:, :9 * C2] = total[:, 18 * C2:27 * C2]
    two[...] = jnp.concatenate([total[:4, 27 * C2:27 * C2 + HALF], total[4:, 27 * C2:27 * C2 + HALF]], axis=1)


def added(blocks):
    total = blocks[0].astype(F32)
    for n in range(1, blocks.shape[0]):
        total = total + blocks[n].astype(F32)
    return lax.optimization_barrier(total)


def from_all(axis, part):
    count = lax.axis_size(axis)
    copies = jnp.broadcast_to(part.astype(BF16)[None], (count,) + part.shape)
    return lax.all_to_all(copies, axis, 0, 0, tiled=True)


def local(feature_one, feature_two, cotangent_three, weight_two, weight_three):
    count = lax.axis_size(SPACE)
    cls = class_matrix()
    to_cls, to_nat = jnp.asarray(cls, BF16), jnp.asarray(cls.T, BF16)
    small = jnp.asarray(np.concatenate(shift_matrices() + (pick_matrix(),), 0), BF16)
    cot = cotangent_three.reshape(C3, L3)
    f1 = feature_one.reshape(C1, X1L, Y1 * Z1).transpose(1, 0, 2)
    layer, f2 = call(
        prepare_kernel, (cot, feature_two.reshape(C2, 2, L2), f1),
        (((C2, L2 + 2 * L3), BF16), ((2 * C2, L2), BF16)), limit=4,
    )
    halo = lax.ppermute(layer, SPACE, [(n, n - 1) for n in range(1, count)])
    own = call(
        own_kernel, (cot, f2, f1, weight_three.T, to_cls, small),
        (((C3, 18 * C2), BF16), ((8 * C2, L3), F32), ((2 * C2, L2), BF16), ((L3, 9 * C2), BF16),
         ((2 * L2, 9 * C1), BF16), ((2 * L2, 9 * C1), BF16), ((12 * C2, 4 * C3), BF16)),
        (pltpu.VMEM((4 * C3, L3), BF16), pltpu.VMEM((48 * C1, 2 * Z1), BF16),
         pltpu.VMEM((9 * C1, 2 * L2), BF16), pltpu.VMEM((9 * C1, 2 * L2), BF16)),
        flops=10**9, moved=4 * 10**6,
    )
    send, back = call(
        joined_kernel, (halo,) + tuple(own) + (to_cls, to_nat, small),
        (((C3, WIDTH), BF16), ((3 * C2, L2), BF16)),
        (pltpu.VMEM((4 * C3, L3), BF16), pltpu.VMEM((C3, HALF), F32)),
    )
    got = lax.all_to_all(send.reshape(count, C3 // count, WIDTH), SPACE, 0, 0, tiled=True)
    (result,) = call(
        activation_kernel, (back, f1, weight_two, jnp.asarray(spread_matrix(), BF16)),
        (((X1L, C1, Y1 * Z1), BF16),),
        (pltpu.VMEM((9 * C2, (Y2 + 1) * Z1), BF16), pltpu.VMEM((12 * C2, 2 * Z2), BF16), pltpu.VMEM((2, 6 * C2, 4 * C1), F32)),
        flops=2 * 10**9, moved=6 * 10**6,
    )
    got = from_all("y", added(from_all("zh", added(got))))
    two, three = call(last_kernel, (got,), (((4, 27 * C1), F32), ((8, 27 * C2), F32)), limit=4)
    return result.transpose(1, 0, 2).reshape(feature_one.shape), two, three


SPACE = ("zl", "x", "core")


def solution(mesh):
    samples = mesh.shape["sample"]
    inner = 8 if samples % 8 == 0 else 1
    fine = Mesh(mesh.devices.reshape(samples // inner, inner, 2, 4, 2), ("zh", "y") + SPACE)
    brick = P(("zh", "y"), None, SPACE, None)
    return jax.shard_map(
        local,
        mesh=fine,
        in_specs=(brick, brick, brick, P(), P()),
        out_specs=(brick, P(SPACE, None), P(SPACE, None)),
        check_vma=False,
    )
```

```python
import jax
import jax.numpy as jnp
import numpy as np
from jax import lax
from jax.experimental import pallas as pl
from jax.experimental.pallas import tpu as pltpu
from jax.sharding import Mesh
from jax.sharding import PartitionSpec as P

F32, BF16 = jnp.float32, jnp.bfloat16
SLOPE = 0.3
X1L, Y1, Z1 = 4, 16, 128
Y2, Z2 = 8, 64
Y3, Z3 = 4, 32
C1, C2, C3 = 32, 64, 128
L2, L3 = Y2 * Z2, Y3 * Z3
HALF = 27 * C1 // 2
WIDTH = 27 * C2 + HALF + 16
CUBES = 32
TAP = {1: (0, 0), 2: (1, 0), 0: (1, 1)}


def class_matrix():
    m = np.zeros((L2, L2), np.float32)
    for y in range(Y2):
        for z in range(Z2):
            m[y * Z2 + z, ((y % 2) * 2 + z % 2) * L3 + (y // 2) * Z3 + z // 2] = 1
    return m


def shift_matrices():
    down = np.zeros((3, L3, L3), np.float32)
    for j in range(Y3):
        for k in range(Z3):
            for n, (dj, dk) in enumerate(((0, 1), (1, 0), (1, 1))):
                if j >= dj and k >= dk:
                    down[n, (j - dj) * Z3 + k - dk, j * Z3 + k] = 1
    up = down.transpose(0, 2, 1)
    return np.concatenate(list(down), 1), np.concatenate(list(up), 1)


def spread_matrix():
    m = np.zeros((2, Z2, 2, 3, Z1), np.float32)
    for h in range(2):
        for c in range(3):
            for k in range(Z2):
                z = 2 * k + c - 1
                if 0 <= z < Z1:
                    m[h, k, h, c, z] = 1
    return m.reshape(2 * Z2, 6 * Z1)


def pick_matrix():
    m = np.zeros((2, Z1, 3, 2, Z2), np.float32)
    for h in range(2):
        for c in range(3):
            for k in range(Z2):
                z = 2 * k + c - 1
                if 0 <= z < Z1:
                    m[h, z, c, h, k] = 1
    return m.reshape(2 * Z1, 6 * Z2)


def dot(a, b):
    return jnp.dot(a, b, preferred_element_type=F32)


def dot_nt(a, b):
    return lax.dot_general(a, b, (((1,), (1,)), ((), ())), preferred_element_type=F32)


def slope(v):
    return jnp.where(v.astype(F32) > 0, 1.0, SLOPE)


def prepare_kernel(cot, f2, _, layer, f2_rows):
    top = f2[:, 0, :]
    layer[:, :L2] = top
    layer[:, L2:L2 + L3] = cot[:C2, :]
    layer[:, L2 + L3:] = cot[C2:, :]
    f2_rows[:C2, :] = top
    f2_rows[C2:, :] = f2[:, 1, :]


def shifts(values, matrices, dst):
    moved = dot(values, matrices).astype(BF16)
    dst[0:C3, :] = values
    for n in range(3):
        dst[(n + 1) * C3:(n + 2) * C3, :] = moved[:, n * L3:(n + 1) * L3]


def own_kernel(cot, f2, f1, w3t, to_cls, small,
               by_tap, totals, act_cls, win_odd, we_t, wo_t, a3, cs, fw, we, wo):
    down, up, pick = small[:L3, :], small[L3:2 * L3, :], small[2 * L3:, :]
    shifts(cot[...], up, cs)
    a3[...] = jnp.zeros_like(a3)
    for a in range(3):
        for b in range(3):
            for c in range(3):
                (q, f), (r, g) = TAP[b], TAP[c]
                rows, cols = (a * 4 + q * 2 + r) * C2, (f * 2 + g) * C3
                tap = (a * 9 + b * 3 + c) * C2
                a3[rows:rows + C2, cols:cols + C3] = w3t[tap:tap + C2, :]
    totals[...] = dot(a3[4 * C2:, :], cs[...])
    f2b = dot(f2[...], to_cls[...]).astype(BF16)
    act_cls[...] = f2b
    cls = [f2b[:, n * L3:(n + 1) * L3] for n in range(4)]
    moved = dot(cls[3], down).astype(BF16)
    by_k, by_j, by_jk = moved[:, :L3], moved[:, L3:2 * L3], moved[:, 2 * L3:]
    row_k = dot(cls[1], down[:, :L3]).astype(BF16)
    col_j = dot(cls[2], down[:, L3:2 * L3]).astype(BF16)
    nine = (by_jk, col_j, by_j, row_k, cls[0], cls[1], by_k, cls[2], cls[3])
    win = [jnp.concatenate([w[x * C2:(x + 1) * C2] for w in nine], axis=0) for x in range(2)]
    win_odd[...] = win[1].T
    by_tap[...] = dot_nt(cot[...], jnp.concatenate(win, axis=0))
    for x in range(4):
        for b in range(3):
            for jp in range(4):
                rows = ((x * 3 + b) * 4 + jp) * C1
                y = 4 * jp + b - 1
                if y < 0:
                    fw[rows:rows + C1, :Z1] = jnp.zeros((C1, Z1), BF16)
                else:
                    fw[rows:rows + C1, :Z1] = f1[x, :, y * Z1:(y + 1) * Z1]
                fw[rows:rows + C1, Z1:] = f1[x, :, (y + 2) * Z1:(y + 3) * Z1]
    picked = dot(fw[...], pick).astype(BF16)
    for x in range(4):
        dst = (we, wo)[x % 2]
        for b in range(3):
            for jp in range(4):
                rows = ((x * 3 + b) * 4 + jp) * C1
                lane = (x // 2) * L2 + jp * 2 * Z2
                for c in range(3):
                    at = (b * 3 + c) * C1
                    dst[at:at + C1, lane:lane + 2 * Z2] = picked[rows:rows + C1, c * 2 * Z2:(c + 1) * 2 * Z2]
    we_t[...] = we[...].T
    wo_t[...] = wo[...].T


def joined_kernel(halo, by_tap, totals, act_cls, win_odd, we_t, wo_t, a3, to_cls, to_nat, small,
                  mine, other, back_out, cs, g2s):
    up = small[L3:2 * L3, :]
    above = jnp.concatenate([halo[:, L2:L2 + L3], halo[:, L2 + L3:]], axis=0)
    shifts(above, up, cs)
    n4 = 4 * C2
    over = dot(a3[:2 * n4, :], cs[...])
    sums = (totals[:n4, :], totals[n4:, :] + over[:n4], over[n4:])
    above_cls = dot(halo[:, :L2], to_cls[...])
    acts = (act_cls[:C2, :], act_cls[C2:, :], above_cls)
    back_cls = []
    for x in range(3):
        tiles = []
        for n in range(4):
            gain = slope(acts[x][:, n * L3:(n + 1) * L3])
            tiles.append((sums[x][n * C2:(n + 1) * C2] * gain).astype(BF16))
        back_cls.append(jnp.concatenate(tiles, axis=1))
    back = dot(jnp.concatenate(back_cls, axis=0), to_nat[...]).astype(BF16)
    back_out[...] = back
    by_tap_above = dot(above, win_odd[...])
    rows3 = [back[x * C2:(x + 1) * C2] for x in range(3)]
    pair = jnp.concatenate([jnp.concatenate([rows3[0], rows3[1]], 1), jnp.concatenate([rows3[1], rows3[2]], 1)], 0)
    even = dot(pair[:C2], we_t[...])
    odd = dot(pair, wo_t[...])
    grad = jnp.concatenate([odd[C2:], even, odd[:C2]], axis=1)
    first, second = grad[:, :HALF], grad[:, HALF:]
    for s in range(C2 // 4):
        g2s[8 * s:8 * s + 4, :] = first[4 * s:4 * s + 4]
        g2s[8 * s + 4:8 * s + 8, :] = second[4 * s:4 * s + 4]
    rows = jnp.concatenate(
        [by_tap[...], by_tap_above, g2s[...], jnp.zeros((C3, WIDTH - 27 * C2 - HALF), F32)], axis=1
    ).reshape(C3 // 16, 2, 8, WIDTH)
    even_core = lax.axis_index("core") == 0
    low, high = rows[:, 0].reshape(C3 // 2, WIDTH), rows[:, 1].reshape(C3 // 2, WIDTH)
    mine[...] = jnp.where(even_core, low, high)
    other[...] = jnp.where(even_core, high, low).astype(BF16)


def activation_kernel(back, f1, w2, spread, out, bu, bk4, w2x):
    rows3 = [back[x * C2:(x + 1) * C2, :] for x in range(3)]
    w2x[...] = jnp.zeros_like(w2x)
    for a in range(3):
        for b in range(3):
            for c in range(3):
                (p, d), (q, f) = TAP[a], TAP[b]
                rows, cols = (d * 3 + c) * C2, (p * 2 + q) * C1
                tap = (a * 9 + b * 3 + c) * C1
                w2x[f, rows:rows + C2, cols:cols + C1] = w2[:, tap:tap + C1].astype(F32)
    w2b = [w2x[f].T.astype(BF16) for f in range(2)]
    for x in range(3):
        for jp in range(4):
            rows = (x * 4 + jp) * C2
            bk4[rows:rows + C2, :] = rows3[x][:, jp * 2 * Z2:(jp + 1) * 2 * Z2]
    wide = dot(bk4[...], spread[...]).astype(BF16)
    bu[:, Y2 * Z1:] = jnp.zeros((9 * C2, Z1), BF16)
    for x in range(3):
        for jp in range(4):
            for h in range(2):
                for c in range(3):
                    rows, at = (x * 4 + jp) * C2, (x * 3 + c) * C2
                    lane, col = (2 * jp + h) * Z1, (h * 3 + c) * Z1
                    bu[at:at + C2, lane:lane + Z1] = wide[rows:rows + C2, col:col + Z1]
    for i in range(2):
        ks = slice(i * 3 * C2, (i + 2) * 3 * C2)
        total = dot(w2b[0], bu[ks, :Y2 * Z1]) + dot(w2b[1], bu[ks, Z1:])
        for p in range(2):
            for q in range(2):
                for j in range(Y2):
                    lanes = pl.ds((2 * j + q) * Z1, Z1)
                    v = total[(p * 2 + q) * C1:(p * 2 + q + 1) * C1, j * Z1:(j + 1) * Z1]
                    out[2 * i + p, :, lanes] = (v * slope(f1[2 * i + p, :, lanes])).astype(BF16)


VM = pl.BlockSpec(memory_space=pltpu.VMEM)


def call(body, args, outs, scratch=(), flops=10**8, moved=10**6, limit=24):
    return pl.pallas_call(
        body,
        out_shape=tuple(jax.ShapeDtypeStruct(shape, dtype) for shape, dtype in outs),
        in_specs=[VM] * len(args),
        out_specs=(VM,) * len(outs),
        scratch_shapes=list(scratch),
        compiler_params=pltpu.CompilerParams(vmem_limit_bytes=limit * 1024 * 1024),
        cost_estimate=pl.CostEstimate(flops=flops, bytes_accessed=moved, transcendentals=0),
    )(*args)


def last_kernel(got, two, three):
    total = got[0].astype(F32)
    for n in range(1, got.shape[0]):
        total = total + got[n].astype(F32)
    total = total * (1.0 / CUBES)
    three[:, 9 * C2:] = total[:, :18 * C2]
    three[:, :9 * C2] = total[:, 18 * C2:27 * C2]
    two[...] = jnp.concatenate([total[:4, 27 * C2:27 * C2 + HALF], total[4:, 27 * C2:27 * C2 + HALF]], axis=1)


def added(blocks):
    total = blocks[0].astype(F32)
    for n in range(1, blocks.shape[0]):
        total = total + blocks[n].astype(F32)
    return lax.optimization_barrier(total)


def from_all(axis, part):
    count = lax.axis_size(axis)
    copies = jnp.broadcast_to(part.astype(BF16)[None], (count,) + part.shape)
    return lax.all_to_all(copies, axis, 0, 0, tiled=True)


def local(feature_one, feature_two, cotangent_three, weight_two, weight_three):
    count = lax.axis_size(SPACE)
    cls = class_matrix()
    to_cls, to_nat = jnp.asarray(cls, BF16), jnp.asarray(cls.T, BF16)
    small = jnp.asarray(np.concatenate(shift_matrices() + (pick_matrix(),), 0), BF16)
    cot = cotangent_three.reshape(C3, L3)
    f1 = feature_one.reshape(C1, X1L, Y1 * Z1).transpose(1, 0, 2)
    layer, f2 = call(
        prepare_kernel, (cot, feature_two.reshape(C2, 2, L2), f1),
        (((C2, L2 + 2 * L3), BF16), ((2 * C2, L2), BF16)), limit=4,
    )
    halo = lax.ppermute(layer, SPACE, [(n, n - 1) for n in range(1, count)])
    own = call(
        own_kernel, (cot, f2, f1, weight_three.T, to_cls, small),
        (((C3, 18 * C2), F32), ((8 * C2, L3), F32), ((2 * C2, L2), BF16), ((L3, 9 * C2), BF16),
         ((2 * L2, 9 * C1), BF16), ((2 * L2, 9 * C1), BF16), ((12 * C2, 4 * C3), BF16)),
        (pltpu.VMEM((4 * C3, L3), BF16), pltpu.VMEM((48 * C1, 2 * Z1), BF16),
         pltpu.VMEM((9 * C1, 2 * L2), BF16), pltpu.VMEM((9 * C1, 2 * L2), BF16)),
        flops=10**9, moved=4 * 10**6,
    )
    mine, other, back = call(
        joined_kernel, (halo,) + tuple(own) + (to_cls, to_nat, small),
        (((C3 // 2, WIDTH), F32), ((C3 // 2, WIDTH), BF16), ((3 * C2, L2), BF16)),
        (pltpu.VMEM((4 * C3, L3), BF16), pltpu.VMEM((C3, HALF), F32)),
    )
    both = mine + lax.ppermute(other, "core", [(0, 1), (1, 0)]).astype(F32)
    got = lax.all_to_all(both.astype(BF16).reshape(count // 2, 8, WIDTH), SPACE[:2], 0, 0, tiled=True)
    (result,) = call(
        activation_kernel, (back, f1, weight_two, jnp.asarray(spread_matrix(), BF16)),
        (((X1L, C1, Y1 * Z1), BF16),),
        (pltpu.VMEM((9 * C2, (Y2 + 1) * Z1), BF16), pltpu.VMEM((12 * C2, 2 * Z2), BF16), pltpu.VMEM((2, 6 * C2, 4 * C1), F32)),
        flops=2 * 10**9, moved=6 * 10**6,
    )
    got = from_all("y", added(from_all("zh", added(got))))
    two, three = call(last_kernel, (got,), (((4, 27 * C1), F32), ((8, 27 * C2), F32)), limit=4)
    return result.transpose(1, 0, 2).reshape(feature_one.shape), two, three


SPACE = ("zl", "x", "core")


def solution(mesh):
    samples = mesh.shape["sample"]
    inner = 8 if samples % 8 == 0 else 1
    fine = Mesh(mesh.devices.reshape(samples // inner, inner, 2, 4, 2), ("zh", "y") + SPACE)
    brick = P(("zh", "y"), None, SPACE, None)
    return jax.shard_map(
        local,
        mesh=fine,
        in_specs=(brick, brick, brick, P(), P()),
        out_specs=(brick, P(SPACE, None), P(SPACE, None)),
        check_vma=False,
    )
```

```python
import jax
import jax.numpy as jnp
import numpy as np
from jax import lax
from jax.experimental import pallas as pl
from jax.experimental.pallas import tpu as pltpu
from jax.sharding import Mesh
from jax.sharding import PartitionSpec as P

F32, BF16 = jnp.float32, jnp.bfloat16
SLOPE = 0.3
X1L, Y1, Z1 = 4, 16, 128
Y2, Z2 = 8, 64
Y3, Z3 = 4, 32
C1, C2, C3 = 32, 64, 128
L2, L3 = Y2 * Z2, Y3 * Z3
HALF = 27 * C1 // 2
WIDTH = 27 * C2 + HALF + 16
CUBES = 32
TAP = {1: (0, 0), 2: (1, 0), 0: (1, 1)}


def class_matrix():
    m = np.zeros((L2, L2), np.float32)
    for y in range(Y2):
        for z in range(Z2):
            m[y * Z2 + z, ((y % 2) * 2 + z % 2) * L3 + (y // 2) * Z3 + z // 2] = 1
    return m


def shift_matrices():
    down = np.zeros((3, L3, L3), np.float32)
    for j in range(Y3):
        for k in range(Z3):
            for n, (dj, dk) in enumerate(((0, 1), (1, 0), (1, 1))):
                if j >= dj and k >= dk:
                    down[n, (j - dj) * Z3 + k - dk, j * Z3 + k] = 1
    up = down.transpose(0, 2, 1)
    return np.concatenate(list(down), 1), np.concatenate(list(up), 1)


def spread_matrix():
    m = np.zeros((2, Z2, 2, 3, Z1), np.float32)
    for h in range(2):
        for c in range(3):
            for k in range(Z2):
                z = 2 * k + c - 1
                if 0 <= z < Z1:
                    m[h, k, h, c, z] = 1
    return m.reshape(2 * Z2, 6 * Z1)


def pick_matrix():
    m = np.zeros((2, Z1, 3, 2, Z2), np.float32)
    for h in range(2):
        for c in range(3):
            for k in range(Z2):
                z = 2 * k + c - 1
                if 0 <= z < Z1:
                    m[h, z, c, h, k] = 1
    return m.reshape(2 * Z1, 6 * Z2)


def dot(a, b):
    return jnp.dot(a, b, preferred_element_type=F32)


def dot_nt(a, b):
    return lax.dot_general(a, b, (((1,), (1,)), ((), ())), preferred_element_type=F32)


def slope(v):
    return jnp.where(v.astype(F32) > 0, 1.0, SLOPE)


def prepare_kernel(cot, f2, _, layer, f2_rows):
    top = f2[:, 0, :]
    layer[:, :L2] = top
    layer[:, L2:L2 + L3] = cot[:C2, :]
    layer[:, L2 + L3:] = cot[C2:, :]
    f2_rows[:C2, :] = top
    f2_rows[C2:, :] = f2[:, 1, :]


def shifts(values, matrices, dst):
    moved = dot(values, matrices).astype(BF16)
    dst[0:C3, :] = values
    for n in range(3):
        dst[(n + 1) * C3:(n + 2) * C3, :] = moved[:, n * L3:(n + 1) * L3]


def by_core(rows, mine, other):
    rows = rows.reshape(C3 // 16, 2, 8, rows.shape[1])
    even_core = lax.axis_index("core") == 0
    low, high = rows[:, 0].reshape(C3 // 2, -1), rows[:, 1].reshape(C3 // 2, -1)
    mine[...] = jnp.where(even_core, low, high)
    other[...] = jnp.where(even_core, high, low).astype(BF16)


def own_kernel(cot, f2, f1, w3t, to_cls, small,
               mine, other, totals, act_cls, win_odd, we_t, wo_t, a3, cs, fw, we, wo):
    down, up, pick = small[:L3, :], small[L3:2 * L3, :], small[2 * L3:, :]
    shifts(cot[...], up, cs)
    a3[...] = jnp.zeros_like(a3)
    for a in range(3):
        for b in range(3):
            for c in range(3):
                (q, f), (r, g) = TAP[b], TAP[c]
                rows, cols = (a * 4 + q * 2 + r) * C2, (f * 2 + g) * C3
                tap = (a * 9 + b * 3 + c) * C2
                a3[rows:rows + C2, cols:cols + C3] = w3t[tap:tap + C2, :]
    totals[...] = dot(a3[4 * C2:, :], cs[...])
    f2b = dot(f2[...], to_cls[...]).astype(BF16)
    act_cls[...] = f2b
    cls = [f2b[:, n * L3:(n + 1) * L3] for n in range(4)]
    moved = dot(cls[3], down).astype(BF16)
    by_k, by_j, by_jk = moved[:, :L3], moved[:, L3:2 * L3], moved[:, 2 * L3:]
    row_k = dot(cls[1], down[:, :L3]).astype(BF16)
    col_j = dot(cls[2], down[:, L3:2 * L3]).astype(BF16)
    nine = (by_jk, col_j, by_j, row_k, cls[0], cls[1], by_k, cls[2], cls[3])
    win = [jnp.concatenate([w[x * C2:(x + 1) * C2] for w in nine], axis=0) for x in range(2)]
    win_odd[...] = win[1].T
    by_core(dot_nt(cot[...], jnp.concatenate(win, axis=0)), mine, other)
    for x in range(4):
        for b in range(3):
            for jp in range(4):
                rows = ((x * 3 + b) * 4 + jp) * C1
                y = 4 * jp + b - 1
                if y < 0:
                    fw[rows:rows + C1, :Z1] = jnp.zeros((C1, Z1), BF16)
                else:
                    fw[rows:rows + C1, :Z1] = f1[x, :, y * Z1:(y + 1) * Z1]
                fw[rows:rows + C1, Z1:] = f1[x, :, (y + 2) * Z1:(y + 3) * Z1]
    picked = dot(fw[...], pick).astype(BF16)
    for x in range(4):
        dst = (we, wo)[x % 2]
        for b in range(3):
            for jp in range(4):
                rows = ((x * 3 + b) * 4 + jp) * C1
                lane = (x // 2) * L2 + jp * 2 * Z2
                for c in range(3):
                    at = (b * 3 + c) * C1
                    dst[at:at + C1, lane:lane + 2 * Z2] = picked[rows:rows + C1, c * 2 * Z2:(c + 1) * 2 * Z2]
    we_t[...] = we[...].T
    wo_t[...] = wo[...].T


def joined_kernel(halo, totals, act_cls, win_odd, we_t, wo_t, a3, to_cls, to_nat, small,
                  mine, other, back_out, cs, g2s):
    up = small[L3:2 * L3, :]
    above = jnp.concatenate([halo[:, L2:L2 + L3], halo[:, L2 + L3:]], axis=0)
    shifts(above, up, cs)
    n4 = 4 * C2
    over = dot(a3[:2 * n4, :], cs[...])
    sums = (totals[:n4, :], totals[n4:, :] + over[:n4], over[n4:])
    above_cls = dot(halo[:, :L2], to_cls[...])
    acts = (act_cls[:C2, :], act_cls[C2:, :], above_cls)
    back_cls = []
    for x in range(3):
        tiles = []
        for n in range(4):
            gain = slope(acts[x][:, n * L3:(n + 1) * L3])
            tiles.append((sums[x][n * C2:(n + 1) * C2] * gain).astype(BF16))
        back_cls.append(jnp.concatenate(tiles, axis=1))
    back = dot(jnp.concatenate(back_cls, axis=0), to_nat[...]).astype(BF16)
    back_out[...] = back
    by_tap_above = dot(above, win_odd[...])
    rows3 = [back[x * C2:(x + 1) * C2] for x in range(3)]
    pair = jnp.concatenate([jnp.concatenate([rows3[0], rows3[1]], 1), jnp.concatenate([rows3[1], rows3[2]], 1)], 0)
    even = dot(pair[:C2], we_t[...])
    odd = dot(pair, wo_t[...])
    grad = jnp.concatenate([odd[C2:], even, odd[:C2]], axis=1)
    first, second = grad[:, :HALF], grad[:, HALF:]
    for s in range(C2 // 4):
        g2s[8 * s:8 * s + 4, :] = first[4 * s:4 * s + 4]
        g2s[8 * s + 4:8 * s + 8, :] = second[4 * s:4 * s + 4]
    by_core(jnp.concatenate(
        [by_tap_above, g2s[...], jnp.zeros((C3, WIDTH - 27 * C2 - HALF), F32)], axis=1
    ), mine, other)


def activation_kernel(back, f1, w2, spread, out, bu, bk4, w2x):
    rows3 = [back[x * C2:(x + 1) * C2, :] for x in range(3)]
    w2x[...] = jnp.zeros_like(w2x)
    for a in range(3):
        for b in range(3):
            for c in range(3):
                (p, d), (q, f) = TAP[a], TAP[b]
                rows, cols = (d * 3 + c) * C2, (p * 2 + q) * C1
                tap = (a * 9 + b * 3 + c) * C1
                w2x[f, rows:rows + C2, cols:cols + C1] = w2[:, tap:tap + C1].astype(F32)
    w2b = [w2x[f].T.astype(BF16) for f in range(2)]
    for x in range(3):
        for jp in range(4):
            rows = (x * 4 + jp) * C2
            bk4[rows:rows + C2, :] = rows3[x][:, jp * 2 * Z2:(jp + 1) * 2 * Z2]
    wide = dot(bk4[...], spread[...]).astype(BF16)
    bu[:, Y2 * Z1:] = jnp.zeros((9 * C2, Z1), BF16)
    for x in range(3):
        for jp in range(4):
            for h in range(2):
                for c in range(3):
                    rows, at = (x * 4 + jp) * C2, (x * 3 + c) * C2
                    lane, col = (2 * jp + h) * Z1, (h * 3 + c) * Z1
                    bu[at:at + C2, lane:lane + Z1] = wide[rows:rows + C2, col:col + Z1]
    for i in range(2):
        ks = slice(i * 3 * C2, (i + 2) * 3 * C2)
        total = dot(w2b[0], bu[ks, :Y2 * Z1]) + dot(w2b[1], bu[ks, Z1:])
        for p in range(2):
            for q in range(2):
                for j in range(Y2):
                    lanes = pl.ds((2 * j + q) * Z1, Z1)
                    v = total[(p * 2 + q) * C1:(p * 2 + q + 1) * C1, j * Z1:(j + 1) * Z1]
                    out[2 * i + p, :, lanes] = (v * slope(f1[2 * i + p, :, lanes])).astype(BF16)


VM = pl.BlockSpec(memory_space=pltpu.VMEM)


def call(body, args, outs, scratch=(), flops=10**8, moved=10**6, limit=24):
    return pl.pallas_call(
        body,
        out_shape=tuple(jax.ShapeDtypeStruct(shape, dtype) for shape, dtype in outs),
        in_specs=[VM] * len(args),
        out_specs=(VM,) * len(outs),
        scratch_shapes=list(scratch),
        compiler_params=pltpu.CompilerParams(vmem_limit_bytes=limit * 1024 * 1024),
        cost_estimate=pl.CostEstimate(flops=flops, bytes_accessed=moved, transcendentals=0),
    )(*args)


def last_kernel(got, two, three):
    total = got[0].astype(F32)
    for n in range(1, got.shape[0]):
        total = total + got[n].astype(F32)
    total = total * (1.0 / CUBES)
    three[:, 9 * C2:] = total[:, :18 * C2]
    three[:, :9 * C2] = total[:, 18 * C2:27 * C2]
    two[...] = jnp.concatenate([total[:4, 27 * C2:27 * C2 + HALF], total[4:, 27 * C2:27 * C2 + HALF]], axis=1)


def added(blocks):
    total = blocks[0].astype(F32)
    for n in range(1, blocks.shape[0]):
        total = total + blocks[n].astype(F32)
    return lax.optimization_barrier(total)


def from_all(axis, part):
    count = lax.axis_size(axis)
    copies = jnp.broadcast_to(part.astype(BF16)[None], (count,) + part.shape)
    return lax.all_to_all(copies, axis, 0, 0, tiled=True)


def local(feature_one, feature_two, cotangent_three, weight_two, weight_three):
    count = lax.axis_size(SPACE)
    cls = class_matrix()
    to_cls, to_nat = jnp.asarray(cls, BF16), jnp.asarray(cls.T, BF16)
    small = jnp.asarray(np.concatenate(shift_matrices() + (pick_matrix(),), 0), BF16)
    cot = cotangent_three.reshape(C3, L3)
    f1 = feature_one.reshape(C1, X1L, Y1 * Z1).transpose(1, 0, 2)
    layer, f2 = call(
        prepare_kernel, (cot, feature_two.reshape(C2, 2, L2), f1),
        (((C2, L2 + 2 * L3), BF16), ((2 * C2, L2), BF16)), limit=4,
    )
    halo = lax.ppermute(layer, SPACE, [(n, n - 1) for n in range(1, count)])
    mine_own, other_own, *own = call(
        own_kernel, (cot, f2, f1, weight_three.T, to_cls, small),
        (((C3 // 2, 18 * C2), F32), ((C3 // 2, 18 * C2), BF16), ((8 * C2, L3), F32), ((2 * C2, L2), BF16), ((L3, 9 * C2), BF16),
         ((2 * L2, 9 * C1), BF16), ((2 * L2, 9 * C1), BF16), ((12 * C2, 4 * C3), BF16)),
        (pltpu.VMEM((4 * C3, L3), BF16), pltpu.VMEM((48 * C1, 2 * Z1), BF16),
         pltpu.VMEM((9 * C1, 2 * L2), BF16), pltpu.VMEM((9 * C1, 2 * L2), BF16)),
        flops=10**9, moved=4 * 10**6,
    )
    swap = [(0, 1), (1, 0)]
    early = lax.ppermute(other_own, "core", swap)
    mine, other, back = call(
        joined_kernel, (halo,) + tuple(own) + (to_cls, to_nat, small),
        (((C3 // 2, WIDTH - 18 * C2), F32), ((C3 // 2, WIDTH - 18 * C2), BF16), ((3 * C2, L2), BF16)),
        (pltpu.VMEM((4 * C3, L3), BF16), pltpu.VMEM((C3, HALF), F32)),
    )
    late = lax.ppermute(other, "core", swap)
    both = jnp.concatenate([mine_own + early.astype(F32), mine + late.astype(F32)], axis=1).astype(BF16)
    got = lax.all_to_all(both.reshape(count // 2, 8, WIDTH), SPACE[:2], 0, 0, tiled=True)
    (result,) = call(
        activation_kernel, (back, f1, weight_two, jnp.asarray(spread_matrix(), BF16)),
        (((X1L, C1, Y1 * Z1), BF16),),
        (pltpu.VMEM((9 * C2, (Y2 + 1) * Z1), BF16), pltpu.VMEM((12 * C2, 2 * Z2), BF16), pltpu.VMEM((2, 6 * C2, 4 * C1), F32)),
        flops=2 * 10**9, moved=6 * 10**6,
    )
    got = from_all("y", added(from_all("zh", added(got))))
    two, three = call(last_kernel, (got,), (((4, 27 * C1), F32), ((8, 27 * C2), F32)), limit=4)
    return result.transpose(1, 0, 2).reshape(feature_one.shape), two, three


SPACE = ("zl", "x", "core")


def solution(mesh):
    samples = mesh.shape["sample"]
    inner = 8 if samples % 8 == 0 else 1
    fine = Mesh(mesh.devices.reshape(samples // inner, inner, 2, 4, 2), ("zh", "y") + SPACE)
    brick = P(("zh", "y"), None, SPACE, None)
    return jax.shard_map(
        local,
        mesh=fine,
        in_specs=(brick, brick, brick, P(), P()),
        out_specs=(brick, P(SPACE, None), P(SPACE, None)),
        check_vma=False,
    )
```
